32 devices in a mesh: seq: 8 (over y, x, core), tp: 4 (over z).
Axes of the slice: x: 2, y: 2, z: 4, core: 2. Of those that a mesh axis runs over, the one named last changes fastest.
Arguments:
- tokens: bfloat16 [8192, 2048], P('seq'), may hold values from -6 to 6
- attn_gain: bfloat16 [2048], P('seq'), may hold values from 0.3984375 to 1.59375
- w_query: bfloat16 [2048, 2048], P('seq', 'tp'), may hold values from -0.125 to 0.125
- w_key: bfloat16 [2048, 2048], P('seq', 'tp'), may hold values from -0.125 to 0.125
- w_value: bfloat16 [2048, 4096], P('seq', 'tp'), may hold values from -0.125 to 0.125
- w_gate_out: bfloat16 [2048, 4096], P('seq', 'tp'), may hold values from -0.125 to 0.125
- w_alpha: bfloat16 [2048, 16], P('seq', 'tp'), may hold values from -0.125 to 0.125
- w_beta: bfloat16 [2048, 16], P('seq', 'tp'), may hold values from -0.125 to 0.125
- conv_query: float32 [4, 2048], P(None, 'tp'), may hold values from -3 to 3
- conv_key: float32 [4, 2048], P(None, 'tp'), may hold values from -3 to 3
- conv_value: float32 [4, 4096], P(None, 'tp'), may hold values from -3 to 3
- decay_scale: float32 [16], P('tp'), may hold values from 0.00012207031 to 0.08
- dt_bias: float32 [16], P('tp'), may hold values from -1 to 1
- out_gain: float32 [256], replicated, may hold values from 0.4 to 1.6
- w_out: bfloat16 [2048, 4096], P('seq', 'tp'), may hold values from -0.15625 to 0.15625
- mlp_gain: bfloat16 [2048], P('seq'), may hold values from 0.3984375 to 1.59375
- w_mlp_gate: bfloat16 [2048, 5504], P('seq', 'tp'), may hold values from -0.125 to 0.125
- w_mlp_up: bfloat16 [2048, 5504], P('seq', 'tp'), may hold values from -0.125 to 0.125
- w_mlp_down: bfloat16 [2048, 5504], P('seq', 'tp'), may hold values from -0.125 to 0.125
- init_state: float32 [16, 128, 256], P('tp'), may hold values from -3 to 3
- seg_starts: int32 [5], replicated, may hold values from 0 to 8128, as said below
- continues: int32 [4], replicated, may hold values 0 or 1
- cotangent: bfloat16 [8192, 2048], P('seq'), may hold values from -6 to 6
Outputs:
- block_out: bfloat16 [8192, 2048], P('seq')
- final_state: float32 [16, 128, 256], P('tp', 'seq')
- grad_tokens: float32 [8192, 2048], P('seq')
- grad_attn_gain: float32 [2048], P('seq')
- grad_w_query: float32 [2048, 2048], P('seq', 'tp')
- grad_w_key: float32 [2048, 2048], P('seq', 'tp')
- grad_w_value: float32 [2048, 4096], P('seq', 'tp')
- grad_w_gate_out: float32 [2048, 4096], P('seq', 'tp')
- grad_w_alpha: float32 [2048, 16], P('seq', 'tp')
- grad_w_beta: float32 [2048, 16], P('seq', 'tp')
- grad_conv_query: float32 [4, 2048], P(None, 'tp')
- grad_conv_key: float32 [4, 2048], P(None, 'tp')
- grad_conv_value: float32 [4, 4096], P(None, 'tp')
- grad_decay_scale: float32 [16], P('tp')
- grad_dt_bias: float32 [16], P('tp')
- grad_out_gain: float32 [256], replicated
- grad_w_out: float32 [2048, 4096], P('seq', 'tp')
- grad_mlp_gain: float32 [2048], P('seq')
- grad_w_mlp_gate: float32 [2048, 5504], P('seq', 'tp')
- grad_w_mlp_up: float32 [2048, 5504], P('seq', 'tp')
- grad_w_mlp_down: float32 [2048, 5504], P('seq', 'tp')
The draws below stay inside these ranges and needn't reach their ends.
Inputs may be any that keep to these rules, and one draw needn't show every extreme that they name: `seg_starts`: strictly increasing multiples of 64: the first is 0, the second lies within the first 1024 tokens, all later ones within the last 1024 tokens of the stream. Entry j is 1 where segment j + 1 continues the document before it (no reset of state or convolution at its start) and 0 where it opens a new document; the first segment always continues from init_state.
All inputs are finite; a program needn't handle non-finite values.
Results may differ from the reference program's by a relative error of at most 0.019.
Values may be sent and summed in bfloat16 or wider, within the bound.
No kernel may reach another device: no remote copies, remote signals or barrier semaphores. Data moves between devices by JAX's collectives and lax.ppermute only.
A program may use at most 384 MiB of HBM per device.

```python
import math
import jax
import jax.numpy as jnp
from jax import lax

D = 2048
HEADS = 16
DK = 128
DV = 256
FF = 5504
GROUP = 64
NSEG = 5
T_DEV = 1024
KD = 2048
VD = 4096
TOKENS = 8192


def draw_seg_starts(key, part):
    per_device = T_DEV // GROUP
    group_total = TOKENS // GROUP
    first_key, second_key = jax.random.split(jax.random.fold_in(key, 17))
    second_start = jax.random.randint(first_key, (1,), 1, per_device).astype(jnp.int32)
    late_picks = jax.random.permutation(second_key, per_device - 1)[:NSEG - 2].astype(jnp.int32)
    late_starts = jnp.sort(late_picks) + (group_total - per_device + 1)
    return jnp.concatenate([jnp.zeros((1,), jnp.int32), second_start, late_starts.astype(jnp.int32)]).astype(jnp.int32) * GROUP


def plant(drawn, key, low, high):
    longest = drawn.shape.index(max(drawn.shape))
    spots = []
    for shift in (0, 1):
        where = [jax.random.randint(jax.random.fold_in(key, axis), (), 0, length) for axis, length in enumerate(drawn.shape)]
        where[longest] = (where[longest] + shift) % drawn.shape[longest]
        spots.append(tuple(where))
    return drawn.at[spots[0]].set(low).at[spots[1]].set(high)


def levels(rng, dims, cuts, smallest, largest):
    level = 1.0
    for position, shards_of in cuts:
        heights = jax.random.uniform(jax.random.fold_in(jax.random.fold_in(rng, 6), position), (shards_of,), jnp.float32, smallest / len(cuts), largest / len(cuts))
        level = level * jnp.repeat(jnp.exp(heights), dims[position] // shards_of).reshape((-1,) + (1,) * (len(dims) - 1 - position))
    return level


def scatter_about(key, shape, spread, reach, cuts=(), kind=jnp.bfloat16):
    values = spread * jax.random.normal(key, shape, jnp.float32)
    if cuts:
        values = values * levels(key, shape, cuts, -0.22, 0.18)
    return jnp.clip(values, -reach, reach).astype(kind)


def setup_inputs(seed: int = 0) -> dict:
    arg_keys = jax.random.split(jax.random.key(seed), 24)
    tokens = scatter_about(arg_keys[0], (TOKENS, D), 1.0, 6.0, ((0, 8),))
    attn_gain = jnp.clip(1.0 + 0.12 * jax.random.normal(arg_keys[1], (D,), jnp.float32), 0.3984375, 1.59375).astype(jnp.bfloat16)
    w_query = scatter_about(arg_keys[2], (D, KD), D ** -0.5, 0.125, ((0, 8), (1, 4)))
    w_key = scatter_about(arg_keys[3], (D, KD), D ** -0.5, 0.125, ((0, 8), (1, 4)))
    w_value = scatter_about(arg_keys[4], (D, VD), D ** -0.5, 0.125, ((0, 8), (1, 4)))
    w_gate_out = scatter_about(arg_keys[5], (D, VD), D ** -0.5, 0.125, ((0, 8), (1, 4)))
    w_alpha = scatter_about(arg_keys[6], (D, HEADS), D ** -0.5, 0.125, ((0, 8), (1, 4)))
    w_beta = scatter_about(arg_keys[7], (D, HEADS), D ** -0.5, 0.125, ((0, 8), (1, 4)))
    conv_query = scatter_about(arg_keys[8], (4, KD), 0.5, 3.0, ((1, 4),), jnp.float32)
    conv_key = scatter_about(arg_keys[9], (4, KD), 0.5, 3.0, ((1, 4),), jnp.float32)
    conv_value = scatter_about(arg_keys[10], (4, VD), 0.5, 3.0, ((1, 4),), jnp.float32)
    decay_scale = jnp.clip(jnp.exp(math.log(0.08) - 6.4851847 * jax.random.uniform(arg_keys[11], (HEADS,), jnp.float32) ** levels(arg_keys[11], (HEADS,), ((0, 4),), -0.2, 0.2)), 0.00012207031, 0.08)
    dt_bias = jnp.clip(jax.random.uniform(arg_keys[12], (HEADS,), jnp.float32, -1.0, 1.0) * levels(arg_keys[12], (HEADS,), ((0, 4),), -0.4, 0.0), -1.0, 1.0)
    out_gain = jnp.clip(1.0 + 0.12 * jax.random.normal(arg_keys[13], (DV,), jnp.float32), 0.4, 1.6)
    w_out = scatter_about(arg_keys[14], (D, VD), (VD // 3) ** -0.5, 0.15625, ((0, 8), (1, 4)))
    mlp_gain = jnp.clip(1.0 + 0.12 * jax.random.normal(arg_keys[15], (D,), jnp.float32), 0.3984375, 1.59375).astype(jnp.bfloat16)
    w_mlp_gate = scatter_about(arg_keys[16], (D, FF), D ** -0.5, 0.125, ((0, 8), (1, 4)))
    w_mlp_up = scatter_about(arg_keys[17], (D, FF), D ** -0.5, 0.125, ((0, 8), (1, 4)))
    w_mlp_down = scatter_about(arg_keys[18], (D, FF), (FF // 3) ** -0.5, 0.125, ((0, 8), (1, 4)))
    init_state = scatter_about(arg_keys[19], (HEADS, DK, DV), 0.5, 3.0, ((0, 4),), jnp.float32)
    seg_starts = draw_seg_starts(jax.random.fold_in(arg_keys[23], 71), 0)
    continues = plant((jax.random.randint(arg_keys[21], (NSEG - 1,), 0, 2) < 1).astype(jnp.int32), jax.random.fold_in(arg_keys[21], 1), 0, 1)
    cotangent = scatter_about(arg_keys[22], (TOKENS, D), 1.0, 6.0, ((0, 8),))
    return dict(tokens=tokens, attn_gain=attn_gain, w_query=w_query, w_key=w_key, w_value=w_value, w_gate_out=w_gate_out, w_alpha=w_alpha, w_beta=w_beta, conv_query=conv_query, conv_key=conv_key, conv_value=conv_value, decay_scale=decay_scale, dt_bias=dt_bias, out_gain=out_gain, w_out=w_out, mlp_gain=mlp_gain, w_mlp_gate=w_mlp_gate, w_mlp_up=w_mlp_up, w_mlp_down=w_mlp_down, init_state=init_state, seg_starts=seg_starts, continues=continues, cotangent=cotangent)


full_precision = lax.Precision.HIGHEST
norm_epsilon = 1e-06
tap_count = 4

@jax.custom_vjp
def low(v):
    return lax.optimization_barrier(v.astype(jnp.bfloat16)).astype(jnp.float32)

@jax.custom_vjp
def low_back(v):
    return v

def low_keep(v):
    return (low(v), None)

def low_pass(kept, grad):
    return (grad,)

def back_keep(v):
    return (v, None)

def back_low(kept, grad):
    return (low(grad),)
low.defvjp(low_keep, low_pass)
low_back.defvjp(back_keep, back_low)

def lower_solve(matrix, rhs):
    return lax.linalg.triangular_solve(matrix, rhs, left_side=True, lower=True, unit_diagonal=True)

def dense(left, right):
    return jnp.dot(left, right, precision=full_precision)

def batch_product(left, right):
    return jnp.einsum('...ij,...jk->...ik', left, right, precision=full_precision)

def rms_scale(values, scales):
    return values * lax.rsqrt(lax.optimization_barrier(jnp.mean(values * values, axis=-1, keepdims=True)) + norm_epsilon) * scales

def doc_numbers(positions, seg_starts, continues):
    opens = (1 - continues).astype(jnp.int32)
    passed = (positions[:, None] >= seg_starts[None, 1:]).astype(jnp.int32)
    return lax.optimization_barrier(jnp.sum(passed * opens[None, :], axis=1))

def tap_masks(positions, seg_starts, continues):
    own_doc = doc_numbers(positions, seg_starts, continues)
    columns = []
    for tap_index in range(tap_count):
        earlier = positions - tap_index
        same_doc = (earlier >= 0) & (doc_numbers(earlier, seg_starts, continues) == own_doc)
        columns.append(same_doc.astype(jnp.float32))
    return jnp.stack(columns, axis=1)

def group_masks(positions, seg_starts, continues):
    firsts = positions[::GROUP]
    same_doc = doc_numbers(firsts, seg_starts, continues) == doc_numbers(firsts - 1, seg_starts, continues)
    return same_doc.astype(jnp.float32)

def conv_silu(features, rim_rows, weights, tap_keep):
    padded = jnp.concatenate([rim_rows, features], axis=0)
    length = features.shape[0]
    total = features * weights[0]
    for tap_index in range(1, tap_count):
        begin = tap_count - 1 - tap_index
        total = total + padded[begin:begin + length] * weights[tap_index] * tap_keep[:, tap_index:tap_index + 1]
    return jax.nn.silu(total)

def unit_rows(values, factor):
    return values * lax.rsqrt(lax.optimization_barrier(jnp.sum(values * values, axis=-1, keepdims=True)) + norm_epsilon) * factor

def mixer_inputs(q_proj, k_proj, v_proj, rim_rows, conv_query, conv_key, conv_value, alpha_proj, beta_proj, decay_scale, dt_bias, tap_keep):
    key_width = q_proj.shape[1]
    head_count = alpha_proj.shape[1]
    length = q_proj.shape[0]
    queries = conv_silu(q_proj, rim_rows[:, :key_width], conv_query, tap_keep)
    key_rows = conv_silu(k_proj, rim_rows[:, key_width:2 * key_width], conv_key, tap_keep)
    value_rows = conv_silu(v_proj, rim_rows[:, 2 * key_width:], conv_value, tap_keep)
    queries = unit_rows(queries.reshape(length, head_count, -1), DK ** (-0.5))
    key_rows = unit_rows(key_rows.reshape(length, head_count, -1), 1.0)
    value_rows = value_rows.reshape(length, head_count, -1)
    log_decay = -decay_scale * jax.nn.softplus(alpha_proj + dt_bias)
    beta_gate = jax.nn.sigmoid(beta_proj)
    return (queries, key_rows, value_rows, log_decay, beta_gate)

def group_rows(values):
    shaped = values.reshape((values.shape[0] // GROUP, GROUP) + values.shape[1:])
    return shaped.transpose(0, 2, 1, 3)

def group_scalars(values):
    shaped = values.reshape((values.shape[0] // GROUP, GROUP) + values.shape[1:])
    return shaped.transpose(0, 2, 1)

def rows_from_groups(values):
    shaped = values.transpose(0, 2, 1, 3)
    return shaped.reshape((shaped.shape[0] * shaped.shape[1],) + shaped.shape[2:])

def group_terms(key_rows, value_rows, log_decay, beta_gate):
    cum_decay = jnp.cumsum(log_decay, axis=-1)
    block_size = log_decay.shape[-1]
    row_ids = lax.broadcasted_iota(jnp.int32, (block_size, block_size), 0)
    col_ids = lax.broadcasted_iota(jnp.int32, (block_size, block_size), 1)
    gap_decay = cum_decay[..., :, None] - cum_decay[..., None, :]
    decay_in = jnp.where(row_ids >= col_ids, jnp.exp(jnp.where(row_ids >= col_ids, gap_decay, 0.0)), 0.0)
    key_gram = jnp.einsum('...ik,...jk->...ij', key_rows, key_rows, precision=full_precision)
    unit_lower = jnp.eye(block_size, dtype=jnp.float32) + jnp.where(row_ids > col_ids, beta_gate[..., :, None] * decay_in * key_gram, 0.0)
    solved_values = lower_solve(unit_lower, beta_gate[..., None] * value_rows)
    solved_keys = lower_solve(unit_lower, (beta_gate * jnp.exp(cum_decay))[..., None] * key_rows)
    key_tail = jnp.exp(cum_decay[..., -1:] - cum_decay)[..., None] * key_rows
    return (cum_decay, decay_in, solved_values, solved_keys, key_tail, key_rows)

def group_apply(carry_state, query_block, parts):
    cum_decay, decay_in, solved_values, solved_keys, key_tail, key_rows = parts
    fresh_values = solved_values - batch_product(solved_keys, carry_state)
    scores = jnp.einsum('...ik,...jk->...ij', query_block, key_rows, precision=full_precision) * decay_in
    block_out = jnp.exp(cum_decay)[..., None] * batch_product(query_block, carry_state) + batch_product(scores, fresh_values)
    new_state = jnp.exp(cum_decay[..., -1])[..., None, None] * carry_state + jnp.einsum('...ck,...cv->...kv', key_tail, fresh_values, precision=full_precision)
    return (new_state, block_out)

def state_pass(start_state, query_blocks, group_parts, keep_group):

    def advance(carry_state, pieces):
        query_block, parts, keep_block = pieces
        return group_apply(carry_state * keep_block, query_block, parts)
    end_state, out_blocks = lax.scan(jax.checkpoint(advance), start_state, (query_blocks, group_parts, keep_group))
    return (out_blocks, end_state)

def gate_norm(out_rows, gate_proj, out_gain):
    normed = rms_scale(out_rows, out_gain)
    return (normed * jax.nn.silu(gate_proj.reshape(out_rows.shape))).reshape(gate_proj.shape)

def reference(tokens, attn_gain, w_query, w_key, w_value, w_gate_out, w_alpha, w_beta, conv_query, conv_key, conv_value, decay_scale, dt_bias, out_gain, w_out, mlp_gain, w_mlp_gate, w_mlp_up, w_mlp_down, init_state, seg_starts, continues, cotangent):
    positions = jnp.arange(TOKENS, dtype=jnp.int32)
    tap_keep = tap_masks(positions, seg_starts, continues)
    keep_group = group_masks(positions, seg_starts, continues)
    rim_zero = jnp.zeros((tap_count - 1, 2 * KD + VD), jnp.float32)

    def forward(tokens_f, attn_gain_f, query_f, key_f, value_f, gate_out_f, alpha_f, beta_f, conv_q_f, conv_k_f, conv_v_f, decay_f, dt_f, out_gain_f, out_f, mlp_gain_f, mlp_gate_f, mlp_up_f, mlp_down_f):
        normed = low(rms_scale(tokens_f, attn_gain_f))
        q_proj = low_back(dense(normed, query_f))
        k_proj = low_back(dense(normed, key_f))
        v_proj = low_back(dense(normed, value_f))
        gate_proj = low_back(dense(normed, gate_out_f))
        alpha_proj = low_back(dense(normed, alpha_f))
        beta_proj = low_back(dense(normed, beta_f))
        queries, key_rows, value_rows, log_decay, beta_gate = mixer_inputs(q_proj, k_proj, v_proj, rim_zero, conv_q_f, conv_k_f, conv_v_f, alpha_proj, beta_proj, decay_f, dt_f, tap_keep)
        parts = group_terms(group_rows(key_rows), group_rows(value_rows), group_scalars(log_decay), group_scalars(beta_gate))
        out_blocks, end_state = state_pass(init_state, group_rows(queries), parts, keep_group)
        gated = low(gate_norm(rows_from_groups(out_blocks), gate_proj, out_gain_f))
        attn = low_back(dense(gated, out_f.T))
        middle = tokens_f + attn
        normed_two = low(rms_scale(middle, mlp_gain_f))
        gate_mlp = low_back(dense(normed_two, mlp_gate_f))
        up_mlp = low_back(dense(normed_two, mlp_up_f))
        hidden = low(jax.nn.silu(gate_mlp) * up_mlp)
        mlp_out = low_back(dense(hidden, mlp_down_f.T))
        return (middle + mlp_out, end_state)
    floats = [item.astype(jnp.float32) for item in (tokens, attn_gain, w_query, w_key, w_value, w_gate_out, w_alpha, w_beta, conv_query, conv_key, conv_value, decay_scale, dt_bias, out_gain, w_out, mlp_gain, w_mlp_gate, w_mlp_up, w_mlp_down)]
    (block_out, final_state), back = jax.vjp(forward, *floats)
    grads = back((cotangent.astype(jnp.float32), jnp.zeros_like(final_state)))
    return (block_out.astype(jnp.bfloat16), final_state, grads[0], grads[1], grads[2], grads[3], grads[4], grads[5], grads[6], grads[7], grads[8], grads[9], grads[10], grads[11], grads[12], grads[13], grads[14], grads[15], grads[16], grads[17], grads[18])
```

```python
from functools import partial

import jax
import jax.numpy as jnp
from jax import lax
from jax.experimental import pallas as pl
from jax.experimental.pallas import tpu as pltpu
from jax.sharding import PartitionSpec as P

DK = 128
DV = 256
DOC_STEP = 64
BLOCK = 128
WIDE = DK + DV
eps = 1e-06
f32 = jnp.float32
bf16 = jnp.bfloat16
CLOSED = -128.0


def low(v):
    return v.astype(bf16)


def mm(a, b):
    return lax.dot_general(low(a), low(b), (((1,), (0,)), ((), ())), preferred_element_type=f32)


def mm_t(a, b):
    return lax.dot_general(low(a), low(b), (((1,), (1,)), ((), ())), preferred_element_type=f32)


def t_mm(a, b):
    return lax.dot_general(low(a), low(b), (((0,), (0,)), ((), ())), preferred_element_type=f32)


def exact_mm(a, b):
    return lax.dot_general(
        a, b, (((1,), (0,)), ((), ())), precision=lax.Precision.HIGHEST, preferred_element_type=f32
    )


def sigmoid(v):
    return 1.0 / (1.0 + jnp.exp(-v))


def square_ids():
    return (
        lax.broadcasted_iota(jnp.int32, (BLOCK, BLOCK), 0),
        lax.broadcasted_iota(jnp.int32, (BLOCK, BLOCK), 1),
    )


def softplus(v):
    return jnp.maximum(v, 0.0) + jnp.log(1.0 + jnp.exp(-jnp.abs(v)))


def decay_rows(ab, hp, keep_a, keep_b, heads):
    lane = lax.broadcasted_iota(jnp.int32, (heads, BLOCK), 1)
    opens = ((lane == 0) & (keep_a < 0.5)) | ((lane == DOC_STEP) & (keep_b < 0.5))
    moved = ab[:heads] + hp[heads:]
    log_decay = jnp.where(opens, CLOSED, -hp[:heads] * softplus(moved))
    return log_decay, sigmoid(ab[heads:]), moved, opens


def to_column(row, diag):
    return jnp.sum(jnp.where(diag, row, 0.0), axis=1, keepdims=True)


def to_row(column, diag):
    return jnp.sum(jnp.where(diag, column, 0.0), axis=0, keepdims=True)


def tap_mask(tap, keep_a, keep_b):
    row = lax.broadcasted_iota(jnp.int32, (BLOCK, DK), 0)
    inner = (row >= DOC_STEP) & (row < DOC_STEP + tap)
    return jnp.where(row < tap, keep_a, jnp.where(inner, keep_b, 1.0))


def tap_mask_back(tap, keep_b):
    row = lax.broadcasted_iota(jnp.int32, (BLOCK, DK), 0)
    return jnp.where((row >= DOC_STEP - tap) & (row < DOC_STEP), keep_b, 1.0)


def conv_total(rows_ref, taps_ref, col, masks):
    cols = slice(col, col + DK)
    total = rows_ref[8 : 8 + BLOCK, cols] * taps_ref[0:1, cols]
    for tap in range(1, 4):
        total = total + rows_ref[8 - tap : 8 - tap + BLOCK, cols] * masks[tap] * taps_ref[
            tap : tap + 1, cols
        ]
    return total


def inverse_lower(a_list, row, col):
    eye = (row == col).astype(f32)
    low_a = [low(a) for a in a_list]
    base = (row >> 3) == (col >> 3)
    x1 = [jnp.where(base, -a, 0.0) for a in a_list]
    x2 = [mm(x, x) for x in x1]
    t = [eye + x + y + mm(x, y) for x, y in zip(x1, x2)]
    x4 = [mm(x, x) for x in x2]
    t = [v + mm(v, x) for v, x in zip(t, x4)]
    for level in (3, 4, 5, 6):
        off = ((row >> (level + 1)) == (col >> (level + 1))) & ((row >> level) != (col >> level))
        part = [mm(jnp.where(off, a, 0.0), v) for a, v in zip(a_list, t)]
        t = [v - mm(v, p) for v, p in zip(t, part)]
    head = [low(v) for v in t]
    tail = [low(v - h.astype(f32)) for v, h in zip(t, head)]
    left = [eye - v - mm(a, h) - mm(a, s) for v, a, h, s in zip(t, low_a, head, tail)]
    return [v + mm(h, r) for v, h, r in zip(t, head, left)]


def load_rows(rows_ref, x_ref, halo_ref, rim_ref, first):
    rows_ref[0:8, :] = jnp.where(first, rim_ref[...], halo_ref[...])
    rows_ref[8 : 8 + BLOCK, :] = x_ref[...]


def unit(v, factor):
    scale = lax.rsqrt(jnp.sum(v * v, axis=1, keepdims=True) + eps) * factor
    return v * scale, scale


def silu(v):
    s = sigmoid(v)
    return v * s, s


def forward_kernel(
    heads,
    keep_ref,
    hp_ref,
    ab_ref,
    x_ref,
    halo_ref,
    rim_ref,
    taps_ref,
    gb_ref,
    t_ref,
    u_ref,
    w_ref,
    pre_ref,
    qf_ref,
    ob_ref,
    map_ref,
    rows_ref,
    state_ref,
):
    c = pl.program_id(0)
    hs = range(heads)
    row, col = square_ids()
    diag = row == col

    @pl.when(c == 0)
    def _():
        for h in hs:
            state_ref[h] = jnp.concatenate(
                [diag.astype(f32), jnp.zeros((DK, DV), f32)], axis=1
            )

    load_rows(rows_ref, x_ref, halo_ref, rim_ref, c == 0)
    keep_a, keep_b = keep_ref[2 * c], keep_ref[2 * c + 1]
    log_decay, beta, _, _ = decay_rows(ab_ref[...], hp_ref[...], keep_a, keep_b, heads)
    cum = exact_mm(log_decay, (row <= col).astype(f32))
    gb_ref[...] = jnp.concatenate([cum, beta], axis=0)
    masks = [None] + [tap_mask(j, keep_a, keep_b) for j in (1, 2, 3)]
    key_at, value_at = heads * DK, 2 * heads * DK

    keys = [
        unit(silu(conv_total(rows_ref, taps_ref, key_at + h * DK, masks))[0], 1.0)[0] for h in hs
    ]
    g_row = [cum[h : h + 1] for h in hs]
    g_col = [to_column(g_row[h], diag) for h in hs]
    b_col = [to_column(beta[h : h + 1], diag) for h in hs]
    decay = [jnp.exp(jnp.where(row >= col, g_col[h] - g_row[h], -1e30)) for h in hs]
    grams = [mm_t(k, k) for k in keys]
    a = [jnp.where(row > col, b_col[h] * decay[h] * grams[h], 0.0) for h in hs]
    t = [low(v) for v in inverse_lower(a, row, col)]
    values = [
        jnp.concatenate(
            [
                silu(conv_total(rows_ref, taps_ref, value_at + h * DV + s * DK, masks))[0]
                for s in range(DV // DK)
            ],
            axis=1,
        )
        for h in hs
    ]
    u = [mm(t[h], b_col[h] * values[h]) for h in hs]
    grow = [jnp.exp(g) for g in g_col]
    w = [low(mm(t[h], (b_col[h] * grow[h]) * keys[h])) for h in hs]
    queries = [
        unit(silu(conv_total(rows_ref, taps_ref, h * DK, masks))[0], DK ** (-0.5))[0] for h in hs
    ]
    scores = [low(mm_t(queries[h], keys[h]) * decay[h]) for h in hs]
    last = [cum[h : h + 1, BLOCK - 1 : BLOCK] for h in hs]
    tail = [low(jnp.exp(last[h] - g_col[h]) * keys[h]) for h in hs]
    state = [state_ref[h] for h in hs]
    low_state = [low(s) for s in state]
    fresh = [
        jnp.concatenate([jnp.zeros((BLOCK, DK), f32), u[h]], axis=1) - mm(w[h], low_state[h])
        for h in hs
    ]
    low_fresh = [low(v) for v in fresh]
    for h in hs:
        new = jnp.exp(last[h]) * state[h] + t_mm(tail[h], low_fresh[h])
        state_ref[h] = new
        map_ref[h] = low(new)
    both = [mm(grow[h] * queries[h], low_state[h]) + mm(scores[h], low_fresh[h]) for h in hs]
    for h in hs:
        t_ref[0, h] = t[h]
        u_ref[:, h * DV : (h + 1) * DV] = low(u[h])
        w_ref[:, h * DK : (h + 1) * DK] = w[h]
        pre_ref[0, h] = low_state[h]
        qf_ref[:, h * DK : (h + 1) * DK] = low(both[h][:, :DK])
        ob_ref[:, h * DV : (h + 1) * DV] = both[h][:, DK:]


def const_spec(shape):
    return pl.BlockSpec(shape, lambda c: (0,) * len(shape))


def params():
    return pltpu.CompilerParams(
        dimension_semantics=("arbitrary",), vmem_limit_bytes=56 * 1024 * 1024
    )


SMEM = pl.BlockSpec(memory_space=pltpu.SMEM)


ANY = pl.BlockSpec(memory_space=pl.ANY)


def ordered(kernel, first, extra):
    def run(*refs):
        return kernel(*refs[:first], *refs[first + extra :])

    return run


def cost(us):
    return pl.CostEstimate(
        flops=int(us * 1.0e9), bytes_accessed=int(us * 1.0e6), transcendentals=0
    )


def forward_local(keep, hp, ab, proj, rim, taps, after=()):
    heads = hp.shape[0] // 2
    length = proj.shape[0]
    blocks = length // BLOCK
    kd, vd = heads * DK, heads * DV
    width = 2 * kd + vd
    shape = jax.ShapeDtypeStruct
    return pl.pallas_call(
        ordered(partial(forward_kernel, heads), 7, len(after)),
        grid=(blocks,),
        in_specs=[
            SMEM,
            const_spec((2 * heads, BLOCK)),
            pl.BlockSpec((2 * heads, BLOCK), lambda c: (0, c)),
            pl.BlockSpec((BLOCK, width), lambda c: (c, 0)),
            pl.BlockSpec((8, width), lambda c: (jnp.maximum(c * (BLOCK // 8) - 1, 0), 0)),
            const_spec((8, width)),
            const_spec((4, width)),
        ]
        + [ANY] * len(after),
        out_specs=[
            pl.BlockSpec((2 * heads, BLOCK), lambda c: (0, c)),
            pl.BlockSpec((1, heads, BLOCK, BLOCK), lambda c: (c, 0, 0, 0)),
            pl.BlockSpec((BLOCK, vd), lambda c: (c, 0)),
            pl.BlockSpec((BLOCK, kd), lambda c: (c, 0)),
            pl.BlockSpec((1, heads, DK, WIDE), lambda c: (c, 0, 0, 0)),
            pl.BlockSpec((BLOCK, kd), lambda c: (c, 0)),
            pl.BlockSpec((BLOCK, vd), lambda c: (c, 0)),
            const_spec((heads, DK, WIDE)),
        ],
        out_shape=[
            shape((2 * heads, length), f32),
            shape((blocks, heads, BLOCK, BLOCK), bf16),
            shape((length, vd), bf16),
            shape((length, kd), bf16),
            shape((blocks, heads, DK, WIDE), bf16),
            shape((length, kd), bf16),
            shape((length, vd), f32),
            shape((heads, DK, WIDE), bf16),
        ],
        scratch_shapes=[
            pltpu.VMEM((8 + BLOCK, width), f32),
            pltpu.VMEM((heads, DK, WIDE), f32),
        ],
        compiler_params=params(),
        cost_estimate=cost(30),
        name="delta_forward",
    )(keep, hp, ab, proj, proj, rim, taps, *after)


def out_norm(ob, qf, start, gain):
    out = ob + mm(qf, start)
    inv = lax.rsqrt(jnp.mean(out * out, axis=1, keepdims=True) + eps)
    return out, inv


def gate_kernel(
    heads, place_ref, maps_ref, init_ref, ob_ref, qf_ref, gate_ref, gain_ref,
    gated_ref, start_ref, final_ref,
):
    c = pl.program_id(0)
    hs = range(heads)

    @pl.when(c == 0)
    def _():
        def step(p, states):
            return tuple(
                mm(maps_ref[p, h, :, :DK], states[h]) + maps_ref[p, h, :, DK:].astype(f32)
                for h in hs
            )

        begin = lax.fori_loop(0, place_ref[0], step, tuple(init_ref[h] for h in hs))
        for h in hs:
            start_ref[h] = begin[h]
        end = lax.fori_loop(place_ref[0], place_ref[1], step, begin)
        for h in hs:
            final_ref[h] = end[h]

    for h in hs:
        vs = slice(h * DV, (h + 1) * DV)
        out, inv = out_norm(
            ob_ref[:, vs], qf_ref[:, h * DK : (h + 1) * DK], start_ref[h], gain_ref[...]
        )
        gated_ref[:, vs] = low(out * inv * gain_ref[...] * silu(gate_ref[:, vs])[0])


def gate_forward(place, maps, init_state, ob, qf, gate_proj, gain, after=()):
    heads = init_state.shape[0]
    length, vd = ob.shape
    kd = heads * DK
    rows = 256
    shape = jax.ShapeDtypeStruct
    return pl.pallas_call(
        ordered(partial(gate_kernel, heads), 7, len(after)),
        grid=(length // rows,),
        in_specs=[
            SMEM,
            const_spec(maps.shape),
            const_spec(init_state.shape),
            pl.BlockSpec((rows, vd), lambda c: (c, 0)),
            pl.BlockSpec((rows, kd), lambda c: (c, 0)),
            pl.BlockSpec((rows, vd), lambda c: (c, gate_proj.shape[1] // vd - 1)),
            const_spec((1, DV)),
        ]
        + [ANY] * len(after),
        out_specs=[
            pl.BlockSpec((rows, vd), lambda c: (c, 0)),
            const_spec(init_state.shape),
            const_spec(init_state.shape),
        ],
        out_shape=[
            shape((length, vd), bf16),
            shape(init_state.shape, f32),
            shape(init_state.shape, f32),
        ],
        compiler_params=params(),
        cost_estimate=cost(10),
        name="gate_forward",
    )(place, maps, init_state, ob, qf, gate_proj, gain, *after)


def gate_back_kernel(
    heads, start_ref, ob_ref, qf_ref, gate_ref, gain_ref, grad_ref,
    dout_ref, dgate_ref, dgain_ref, lead_ref, total_ref,
):
    c = pl.program_id(0)

    @pl.when(c == 0)
    def _():
        dgain_ref[...] = jnp.zeros_like(dgain_ref)
        total_ref[...] = jnp.zeros_like(total_ref)

    gain = gain_ref[...]
    for h in range(heads):
        vs = slice(h * DV, (h + 1) * DV)
        qf = qf_ref[:, h * DK : (h + 1) * DK]
        out, inv = out_norm(ob_ref[:, vs], qf, start_ref[h], gain)
        gate = gate_ref[:, vs]
        act, s = silu(gate)
        grad = grad_ref[:, vs].astype(f32)
        hat = out * inv
        dn = grad * act
        dgate_ref[:, vs] = low(grad * hat * gain * (s * (1.0 + gate * (1.0 - s))))
        part = dn * hat
        rows = part.shape[0]
        dgain_ref[...] += jnp.sum(part.reshape(rows // 8, 8, DV), axis=0)
        dh = dn * gain
        dout = low(inv * (dh - hat * jnp.mean(dh * hat, axis=1, keepdims=True)))
        dout_ref[:, vs] = dout
        total_ref[h] += t_mm(qf, dout)

    @pl.when(c == pl.num_programs(0) - 1)
    def _():
        lead_ref[...] = low(total_ref[...])


def gate_backward(start, ob, qf, gate_proj, gain, grad, after=()):
    heads = start.shape[0]
    length, vd = ob.shape
    kd = heads * DK
    rows = 256
    shape = jax.ShapeDtypeStruct
    block_v = pl.BlockSpec((rows, vd), lambda c: (c, 0))
    return pl.pallas_call(
        ordered(partial(gate_back_kernel, heads), 6, len(after)),
        grid=(length // rows,),
        in_specs=[
            const_spec(start.shape),
            block_v,
            pl.BlockSpec((rows, kd), lambda c: (c, 0)),
            pl.BlockSpec((rows, vd), lambda c: (c, gate_proj.shape[1] // vd - 1)),
            const_spec((1, DV)),
            block_v,
        ]
        + [ANY] * len(after),
        out_specs=[
            block_v,
            pl.BlockSpec((rows, vd), lambda c: (c, 2 * kd // vd + 1)),
            const_spec((8, DV)),
            const_spec(start.shape),
        ],
        out_shape=[
            shape((length, vd), bf16),
            shape((length, 2 * kd + 2 * vd), bf16),
            shape((8, DV), f32),
            shape(start.shape, bf16),
        ],
        scratch_shapes=[pltpu.VMEM(start.shape, f32)],
        compiler_params=params(),
        cost_estimate=cost(11),
        name="gate_backward",
    )(start, ob, qf, gate_proj, gain, grad, *after)


def eights(v):
    return jnp.sum(v.reshape(v.shape[0] // 8, 8, v.shape[1]), axis=0)


def backward_kernel(
    heads, blocks,
    place_ref, keep_ref, hp_ref, ab_ref, x_ref, halo_ref, rim_ref, taps_ref,
    gb_ref, t_ref, u_ref, w_ref, pre_ref, dout_ref, start_ref, maps_ref, leads_ref,
    dx_ref, dlast_ref, drim_ref, dab_ref, dtaps_ref, dhp_ref,
    rows_ref, grads_ref, dstate_ref,
):
    step = pl.program_id(0)
    c = blocks - 1 - step
    hs = range(heads)
    row, col = square_ids()
    diag = row == col
    key_at, value_at = heads * DK, 2 * heads * DK

    @pl.when(step == 0)
    def _():
        me, count = place_ref[0], place_ref[1]

        def relay(i, grads):
            p = count - 1 - i
            return tuple(
                t_mm(maps_ref[p, h, :, :DK], grads[h]) + leads_ref[p - me - 1, h].astype(f32) for h in hs
            )

        end = lax.fori_loop(
            0, count - 1 - me, relay, tuple(jnp.zeros((DK, DV), f32) for h in hs)
        )
        for h in hs:
            dstate_ref[h] = end[h]
        grads_ref[BLOCK:, :] = jnp.zeros_like(grads_ref[BLOCK:, :])
        dtaps_ref[...] = jnp.zeros_like(dtaps_ref)
        dhp_ref[...] = jnp.zeros_like(dhp_ref)

    load_rows(rows_ref, x_ref, halo_ref, rim_ref, c == 0)
    keep_a, keep_b = keep_ref[2 * c], keep_ref[2 * c + 1]
    log_decay, beta, moved, opens = decay_rows(ab_ref[...], hp_ref[...], keep_a, keep_b, heads)
    cum = gb_ref[:heads]
    masks = [None] + [tap_mask(j, keep_a, keep_b) for j in (1, 2, 3)]
    masks_back = [None] + [tap_mask_back(j, keep_b) for j in (1, 2, 3)]

    q_sum = [conv_total(rows_ref, taps_ref, h * DK, masks) for h in hs]
    k_sum = [conv_total(rows_ref, taps_ref, key_at + h * DK, masks) for h in hs]
    q_act = [silu(v) for v in q_sum]
    k_act = [silu(v) for v in k_sum]
    q_unit = [unit(v[0], DK ** (-0.5)) for v in q_act]
    k_unit = [unit(v[0], 1.0) for v in k_act]
    queries = [v[0] for v in q_unit]
    keys = [v[0] for v in k_unit]
    low_q = [low(v) for v in queries]
    low_k = [low(v) for v in keys]
    g_row = [cum[h : h + 1] for h in hs]
    g_col = [to_column(g_row[h], diag) for h in hs]
    b_col = [to_column(beta[h : h + 1], diag) for h in hs]
    grow = [jnp.exp(v) for v in g_col]
    last = [cum[h : h + 1, BLOCK - 1 : BLOCK] for h in hs]
    tail = [jnp.exp(last[h] - g_col[h]) for h in hs]
    decay = [jnp.exp(jnp.where(row >= col, g_col[h] - g_row[h], -1e30)) for h in hs]
    grams = [mm_t(k, k) for k in low_k]
    raw = [mm_t(low_q[h], low_k[h]) for h in hs]
    scores = [low(raw[h] * decay[h]) for h in hs]
    begin = [low(start_ref[h]) for h in hs]
    state = [
        mm(pre_ref[0, h, :, :DK], begin[h]) + pre_ref[0, h, :, DK:].astype(f32) for h in hs
    ]
    low_state = [low(v) for v in state]
    u = [u_ref[:, h * DV : (h + 1) * DV] for h in hs]
    w = [w_ref[:, h * DK : (h + 1) * DK] for h in hs]
    t = [t_ref[0, h] for h in hs]
    fresh = [low(u[h].astype(f32) - mm(w[h], low_state[h])) for h in hs]
    dout = [dout_ref[:, h * DV : (h + 1) * DV] for h in hs]
    dstate = [dstate_ref[h] for h in hs]
    low_dstate = [low(v) for v in dstate]
    key_tail = [tail[h] * keys[h] for h in hs]
    dfresh = [t_mm(scores[h], dout[h]) + mm(key_tail[h], low_dstate[h]) for h in hs]
    low_df = [low(v) for v in dfresh]
    q_grow = [grow[h] * queries[h] for h in hs]
    for h in hs:
        dstate_ref[h] = (
            jnp.exp(last[h]) * dstate[h] + t_mm(q_grow[h], dout[h]) - t_mm(w[h], low_df[h])
        )
    dscores = [mm_t(dout[h], fresh[h]) for h in hs]
    dq_grow = [mm_t(dout[h], low_state[h]) for h in hs]
    dk_tail = [mm_t(fresh[h], low_dstate[h]) for h in hs]
    dw = [-mm_t(low_df[h], low_state[h]) for h in hs]
    r_value = [t_mm(t[h], low_df[h]) for h in hs]
    r_key = [t_mm(t[h], dw[h]) for h in hs]
    da = [
        jnp.where(row > col, -(mm_t(r_value[h], u[h]) + mm_t(r_key[h], w[h])), 0.0) for h in hs
    ]
    dsd = [dscores[h] * decay[h] for h in hs]
    dad = [da[h] * decay[h] for h in hs]
    mixed = [dad[h] * grams[h] for h in hs]
    both = [b_col[h] * mixed[h] + dsd[h] * raw[h] for h in hs]
    lift = [b_col[h] * grow[h] for h in hs]
    low_dsd = [low(v) for v in dsd]
    hmat = [b_col[h] * dad[h] for h in hs]
    dq = [grow[h] * dq_grow[h] + mm(low_dsd[h], low_k[h]) for h in hs]
    dk = [
        t_mm(low_dsd[h], low_q[h])
        + tail[h] * dk_tail[h]
        + lift[h] * r_key[h]
        + mm(hmat[h], low_k[h])
        + t_mm(hmat[h], low_k[h])
        for h in hs
    ]

    cum_parts, beta_parts = [], []
    for h in hs:
        rk = jnp.sum(r_key[h] * keys[h], axis=1, keepdims=True)
        tails = jnp.sum(dk_tail[h] * key_tail[h], axis=1, keepdims=True)
        part = (
            jnp.sum(both[h], axis=1, keepdims=True)
            + jnp.sum(dq_grow[h] * q_grow[h], axis=1, keepdims=True)
            + lift[h] * rk
            - tails
        )
        end_part = jnp.sum(tails, axis=0, keepdims=True) + jnp.exp(last[h]) * jnp.sum(
            jnp.sum(dstate[h] * state[h], axis=1, keepdims=True), axis=0, keepdims=True
        )
        dcum = to_row(part, diag) - jnp.sum(both[h], axis=0, keepdims=True)
        lane = lax.broadcasted_iota(jnp.int32, (1, BLOCK), 1)
        cum_parts.append(dcum + jnp.where(lane == BLOCK - 1, end_part, 0.0))
        beta_parts.append(
            jnp.sum(mixed[h], axis=1, keepdims=True) + grow[h] * rk
        )

    def conv_back(dact, total, s, at):
        dtot = dact * (s * (1.0 + total * (1.0 - s)))
        cols = slice(at, at + DK)
        grads_ref[0:BLOCK, cols] = dtot
        dtaps_ref[0, :, cols] += eights(dtot * rows_ref[8 : 8 + BLOCK, cols])
        dx = dtot * taps_ref[0:1, cols]
        for j in (1, 2, 3):
            dtaps_ref[j, :, cols] += eights(
                dtot * masks[j] * rows_ref[8 - j : 8 - j + BLOCK, cols]
            )
            dx = dx + grads_ref[j : j + BLOCK, cols] * masks_back[j] * taps_ref[j : j + 1, cols]
        dx_ref[:, cols] = low(dx)

        @pl.when(step == 0)
        def _():
            dlast_ref[:, cols] = dx[BLOCK - 8 :]

        grads_ref[BLOCK : BLOCK + 8, cols] = dtot[0:8] * keep_a

    def unit_back(grad, normal, scale, factor):
        inner = jnp.sum(grad * normal, axis=1, keepdims=True) * (1.0 / (factor * factor))
        return scale * (grad - normal * inner)

    for h in hs:
        conv_back(
            unit_back(dq[h], queries[h], q_unit[h][1], DK ** (-0.5)),
            q_sum[h], q_act[h][1], h * DK,
        )
        conv_back(
            unit_back(dk[h], keys[h], k_unit[h][1], 1.0), k_sum[h], k_act[h][1], key_at + h * DK
        )
        dot_v = 0.0
        for s in range(DV // DK):
            at = value_at + h * DV + s * DK
            total = conv_total(rows_ref, taps_ref, at, masks)
            act, sig = silu(total)
            rv = r_value[h][:, s * DK : (s + 1) * DK]
            dot_v = dot_v + jnp.sum(rv * act, axis=1, keepdims=True)
            conv_back(b_col[h] * rv, total, sig, at)
        beta_parts[h] = to_row(beta_parts[h] + dot_v, diag)

    dcum = jnp.concatenate(cum_parts, axis=0)
    dlog = jnp.where(opens, 0.0, exact_mm(dcum, (row >= col).astype(f32)))
    dbeta = jnp.concatenate(beta_parts, axis=0)
    dalpha = -dlog * hp_ref[:heads] * sigmoid(moved)
    dab_ref[...] = jnp.concatenate([dalpha, dbeta * beta * (1.0 - beta)], axis=0)
    dhp_ref[...] += jnp.concatenate([-dlog * softplus(moved), dalpha], axis=0)

    @pl.when(step == blocks - 1)
    def _():
        grads_ref[BLOCK - 8 : BLOCK, :] = jnp.zeros((8, grads_ref.shape[1]), f32)
        total = jnp.zeros((8, grads_ref.shape[1]), f32)
        for j in (1, 2, 3):
            total = total + grads_ref[BLOCK - 8 + j : BLOCK + j, :] * taps_ref[j : j + 1, :]
        drim_ref[...] = total


def backward_local(
    place, keep, hp, ab, proj, rim, taps, gb, t, u, w, pre, dout, start, maps, leads, grads,
    after=(),
):
    heads = hp.shape[0] // 2
    length = proj.shape[0]
    blocks = length // BLOCK
    kd, vd = heads * DK, heads * DV
    width = 2 * kd + vd
    shape = jax.ShapeDtypeStruct
    back = blocks - 1
    eighth = BLOCK // 8
    return pl.pallas_call(
        ordered(partial(backward_kernel, heads, blocks), 17, 1 + len(after)),
        grid=(blocks,),
        in_specs=[
            SMEM,
            SMEM,
            const_spec((2 * heads, BLOCK)),
            pl.BlockSpec((2 * heads, BLOCK), lambda c: (0, back - c)),
            pl.BlockSpec((BLOCK, width), lambda c: (back - c, 0)),
            pl.BlockSpec((8, width), lambda c: (jnp.maximum((back - c) * eighth - 1, 0), 0)),
            const_spec((8, width)),
            const_spec((4, width)),
            pl.BlockSpec((2 * heads, BLOCK), lambda c: (0, back - c)),
            pl.BlockSpec((1, heads, BLOCK, BLOCK), lambda c: (back - c, 0, 0, 0)),
            pl.BlockSpec((BLOCK, vd), lambda c: (back - c, 0)),
            pl.BlockSpec((BLOCK, kd), lambda c: (back - c, 0)),
            pl.BlockSpec((1, heads, DK, WIDE), lambda c: (back - c, 0, 0, 0)),
            pl.BlockSpec((BLOCK, vd), lambda c: (back - c, 0)),
            const_spec(start.shape),
            const_spec(maps.shape),
            const_spec(leads.shape),
        ]
        + [ANY] * (1 + len(after)),
        out_specs=[
            pl.BlockSpec((BLOCK, width), lambda c: (back - c, 0)),
            const_spec((8, width)),
            const_spec((8, width)),
            pl.BlockSpec((2 * heads, BLOCK), lambda c: (0, back - c)),
            const_spec((4, 8, width)),
            const_spec((2 * heads, BLOCK)),
        ],
        out_shape=[
            shape(grads.shape, bf16),
            shape((8, width), f32),
            shape((8, width), f32),
            shape((2 * heads, length), f32),
            shape((4, 8, width), f32),
            shape((2 * heads, BLOCK), f32),
        ],
        scratch_shapes=[
            pltpu.VMEM((8 + BLOCK, width), f32),
            pltpu.VMEM((8 + BLOCK, width), f32),
            pltpu.VMEM(start.shape, f32),
        ],
        compiler_params=params(),
        input_output_aliases={17: 0},
        cost_estimate=cost(50),
        name="delta_backward",
    )(
        place, keep, hp, ab, proj, proj, rim, taps, gb, t, u, w, pre, dout, start, maps, leads,
        grads, *after,
    )


def tie(block, *after):
    return pl.pallas_call(
        lambda *refs: None,
        in_specs=[ANY] * (1 + len(after)),
        out_specs=ANY,
        out_shape=jax.ShapeDtypeStruct(block.shape, block.dtype),
        input_output_aliases={0: 0},
        cost_estimate=cost(1),
        name="tie",
    )(block, *after)


def swiglu_kernel(units, gate_ref, up_ref, grad_ref, hidden_ref, grads_ref):
    gate, up = gate_ref[...], up_ref[...]
    act, s = silu(gate)
    hidden_ref[...] = low(act * up)
    grad = grad_ref[...].astype(f32)
    grads_ref[:, :units] = low(grad * up * (s * (1.0 + gate * (1.0 - s))))
    grads_ref[:, units:] = low(grad * act)


def swiglu_both(gate, up, grad):
    rows, units = grad.shape
    step = 64
    spec = lambda columns: pl.BlockSpec((step, columns), lambda c: (c, 0))
    shape = jax.ShapeDtypeStruct
    return pl.pallas_call(
        partial(swiglu_kernel, units),
        grid=(rows // step,),
        in_specs=[spec(units)] * 3,
        out_specs=[spec(units), spec(2 * units)],
        out_shape=[shape((rows, units), bf16), shape((rows, 2 * units), bf16)],
        compiler_params=params(),
        cost_estimate=cost(8),
        name="swiglu_both",
    )(gate, up, grad)


def rms_scale(values, scales):
    return (
        values * lax.rsqrt(jnp.mean(values * values, axis=-1, keepdims=True) + eps) * scales
    )


def doc_numbers(positions, seg_starts, continues):
    opens = 1 - continues
    passed = (positions[:, None] >= seg_starts[None, 1:]).astype(jnp.int32)
    return jnp.sum(passed * opens[None, :], axis=1)


def passed_along(block, axis, distance):
    devices = range(lax.axis_size(axis))
    route = [(i - distance, i) for i in devices if i - distance in devices]
    return lax.ppermute(block, axis, route)


def rows_times(left, right):
    return jnp.dot(left, right, preferred_element_type=f32)


def times_back(left, right):
    return jnp.einsum("tc,dc->td", left, right, preferred_element_type=f32)


def weight_grad(left, right):
    return low(jnp.einsum("td,tc->dc", left, right, preferred_element_type=f32))


def gather_rows(block, axis="seq"):
    return lax.all_gather(block, axis, axis=0, tiled=True)


def scatter_rows(block, axis="seq"):
    return lax.psum_scatter(low(block), axis, scatter_dimension=0, tiled=True)


def next_hop(pair, axis, step):
    n = lax.axis_size(axis)
    return (
        lax.ppermute(pair[0], axis, [(i, i + 1) for i in range(step, n - 1)]),
        lax.ppermute(pair[1], axis, [(n - 1 - i, n - 2 - i) for i in range(step, n - 1)]),
    )


def line_steps(rows, axis):
    n = lax.axis_size(axis)
    me = lax.axis_index(axis)
    own = rows.shape[0] // n
    chunk = lambda at: lax.dynamic_slice_in_dim(rows, jnp.clip(at, 0, n - 1) * own, own, 0)

    def payload(step, came):
        up, down = chunk(n - 1 + me - step), chunk(me - (n - 1) + step)
        if came is None:
            return up, down
        return low(up.astype(f32) + came[0].astype(f32)), low(
            down.astype(f32) + came[1].astype(f32)
        )

    def send(step, pair):
        return (
            lax.ppermute(pair[0], axis, [(i, i + 1) for i in range(step + 1)]),
            lax.ppermute(pair[1], axis, [(n - 1 - i, n - 2 - i) for i in range(step + 1)]),
        )

    return payload, send, lambda came: (
        chunk(me).astype(f32) + came[0].astype(f32) + came[1].astype(f32)
    )


def line_scatter(rows, axis):
    payload, send, total = line_steps(rows, axis)
    came = None
    for step in range(lax.axis_size(axis) - 1):
        came = send(step, payload(step, came))
    return total(came)


def assembled(block, came, axis):
    n = lax.axis_size(axis)
    me = lax.axis_index(axis)
    own = block.shape[0]
    out = jnp.zeros((n * own,) + block.shape[1:], block.dtype)
    put = lambda out, part, at: lax.dynamic_update_slice_in_dim(
        out, part, jnp.clip(at, 0, n - 1) * own, 0
    )
    for step in range(n - 2, -1, -1):
        right, left = came[step]
        out = put(put(out, right, me - 1 - step), left, me + 1 + step)
    return put(out, block, me)


def line_gather(block, axis):
    came = [(block, block)]
    for step in range(lax.axis_size(axis) - 1):
        came.append(next_hop(came[-1], axis, step))
    return assembled(block, came[1:], axis)


def swapped(block, axis, bit):
    return lax.ppermute(block, axis, [(i, i ^ bit) for i in range(lax.axis_size(axis))])


def exchange_step(values, axis, step):
    return values + swapped(values, axis, 1 << step)


def tree_sum(values, axis, first):
    for step in range(first, lax.axis_size(axis).bit_length() - 1):
        values = exchange_step(values, axis, step)
    return values


def body(
    tokens, attn_gain, w_query, w_key, w_value, w_gate_out, w_alpha, w_beta,
    conv_query, conv_key, conv_value, decay_scale, dt_bias, out_gain, w_out, mlp_gain,
    w_mlp_gate, w_mlp_up, w_mlp_down, init_state, seg_starts, continues, cotangent,
):
    count = lax.axis_size("seq")
    me = lax.axis_index("seq")
    lane = lax.axis_index("tp")
    length, width = tokens.shape
    heads = decay_scale.shape[0]
    kd, vd = heads * DK, heads * DV
    own = length // lax.axis_size("tp")
    rows_of = lambda rows, at: lax.dynamic_slice_in_dim(rows, at * own, own, 0)
    mine = lambda rows: rows_of(rows, lane)
    pair = lambda rows: jnp.concatenate([rows_of(rows, lane), rows_of(rows, lane ^ 1)], axis=0)

    after = lambda pair, *awaited: [tie(v, *awaited) for v in pair]

    units = w_mlp_gate.shape[1]
    fill = jnp.zeros((w_mlp_gate.shape[0], -units % 128), bf16)
    half_units = units + fill.shape[1]
    all_units = 2 * half_units
    other_down = swapped(w_mlp_down, "tp", 2)
    other_gate = swapped(w_mlp_gate, "tp", 2)
    first_part = units * 2 // 7 // 128 * 128
    other_up = [
        swapped(w_mlp_up[:, :first_part], "tp", 2),
        swapped(w_mlp_up[:, first_part:], "tp", 2),
    ]
    small = gather_rows(
        jnp.concatenate(
            [w_alpha, w_beta, attn_gain[:, None], mlp_gain[:, None]]
            + [jnp.zeros((w_alpha.shape[0], 6), bf16)],
            axis=1,
        )
    )
    full_ab = small[:, : 2 * heads]
    gain_one = small[:, 2 * heads].astype(f32)
    gain_two = small[:, 2 * heads + 1].astype(f32)
    full_qkv = gather_rows(jnp.concatenate([w_query, w_key, w_value], axis=1))
    full_go = gather_rows(jnp.concatenate([w_gate_out, w_out], axis=1))
    full_gate, full_out = full_go[:, :vd], full_go[:, vd:]
    full_dg = gather_rows(
        jnp.concatenate(
            [w_mlp_down, fill, other_down, fill, w_mlp_gate, fill, other_gate, fill], axis=1
        )
    )
    full_down, full_mlp_gate = full_dg[:, :all_units], full_dg[:, all_units:]

    firsts = me * length + DOC_STEP * jnp.arange(length // DOC_STEP, dtype=jnp.int32)
    keep = (
        doc_numbers(firsts, seg_starts, continues)
        == doc_numbers(firsts - 1, seg_starts, continues)
    ).astype(f32)
    place = jnp.stack([me, jnp.int32(count)]).astype(jnp.int32)
    hp = jnp.broadcast_to(jnp.concatenate([decay_scale, dt_bias])[:, None], (2 * heads, BLOCK))
    taps = jnp.concatenate([conv_query, conv_key, conv_value], axis=1)
    gain_row = out_gain[None, :]

    normed = low(rms_scale(tokens.astype(f32), gain_one))
    proj = rows_times(normed, full_qkv)
    ab = jnp.einsum("dc,td->ct", full_ab, normed, preferred_element_type=f32)
    gate_proj = rows_times(normed, full_gate)
    rim = passed_along(proj[-8:], "seq", 1)
    gb, t_inv, u, w, pre, qf, ob, own_map = forward_local(
        keep, hp, ab, proj, rim, taps, (other_down, other_gate, other_up[0])
    )
    maps = lax.all_gather(own_map, "seq", axis=0)
    gated, start, final = gate_forward(
        place, maps, init_state, ob, qf, gate_proj, gain_row
    )
    full_mlp_up = gather_rows(jnp.concatenate([w_mlp_up, fill, *other_up, fill], axis=1))
    piece = final.shape[1] // count
    final_state = lax.dynamic_slice_in_dim(final, me * piece, piece, 1)

    middle = mine(tokens).astype(f32) + line_scatter(low(times_back(gated, full_out)), "tp")
    normed_two_f, norm_two_back = jax.vjp(rms_scale, middle, gain_two)
    own_two = low(normed_two_f)
    normed_two = jnp.concatenate([own_two, swapped(own_two, "tp", 1)], axis=0)
    cot_pair = pair(cotangent)
    grad_hidden = low(rows_times(cot_pair, full_down))
    gate_mlp = rows_times(normed_two, full_mlp_gate)
    up_mlp = rows_times(tie(normed_two, gate_mlp, grad_hidden), full_mlp_up)
    hidden, grad_both = swiglu_both(gate_mlp, up_mlp, grad_hidden)
    grad_two_part = times_back(grad_both[:, :all_units], full_mlp_gate) + times_back(
        grad_both[:, all_units:], full_mlp_up
    )
    part_two = low(grad_two_part[own:])
    part_two = swapped(part_two, "tp", 1)
    grad_two = grad_two_part[:own] + part_two.astype(f32)
    term_both = tie(weight_grad(normed_two, grad_both), part_two)
    grad_middle_norm, grad_mlp_gain_part = norm_two_back(grad_two)
    grad_middle = mine(cotangent).astype(f32) + grad_middle_norm
    own_attn = tie(low(grad_middle), term_both)
    grad_w_both = scatter_rows(term_both)
    mlp_part = times_back(hidden, full_down)
    part_back = low(mlp_part[own:])
    term_down = weight_grad(cot_pair, hidden)
    came = [next_hop((own_attn, own_attn), "tp", 0)]
    came.append(next_hop(after(came[0], part_back), "tp", 1))
    came.append(next_hop(after(came[1], term_down), "tp", 2))
    grad_attn = assembled(own_attn, came, "tp")

    grad_gated = rows_times(grad_attn, full_out)
    dout, d_all, dgain, lead = gate_backward(
        start, ob, qf, gate_proj, gain_row, grad_gated, (part_back, term_down)
    )
    leads = [passed_along(lead, "seq", -d) for d in range(1, count)]
    grad_w_down = scatter_rows(term_down)
    term_out = weight_grad(tie(grad_attn, leads[0]), gated)
    grad_w_out = scatter_rows(term_out)
    part_back = swapped(tie(part_back, grad_attn), "tp", 1)
    block_own = low(middle + mlp_part[:own] + part_back.astype(f32))
    d_all, dlast, drim, dab, dtaps, dhp = backward_local(
        place, keep, hp, ab, proj, rim, taps, gb, t_inv, u, w, pre, dout, start, maps,
        jnp.stack(leads),
        d_all, (term_out, block_own),
    )
    came = [next_hop((block_own, block_own), "tp", 0)]
    back_gate = swapped(grad_w_both[:, half_units:all_units], "tp", 2)
    d_all = tie(d_all, *came[0], back_gate)
    back_up = swapped(tie(grad_w_both[:, all_units + half_units :], d_all), "tp", 2)

    fixed = low(dlast + passed_along(drim, "seq", -1))
    d_all = lax.dynamic_update_slice(d_all, fixed, (length - 8, 0))
    dab = low(dab)
    wide = taps.shape[1]
    grad_normed = (
        times_back(d_all[:, :wide], full_qkv)
        + times_back(d_all[:, wide:], full_gate)
        + jnp.einsum("ct,dc->td", dab, full_ab, preferred_element_type=f32)
    )
    tokens_f = tokens.astype(f32)
    grad_attn_gain_part = jnp.sum(
        grad_normed
        * (tokens_f * lax.rsqrt(jnp.mean(tokens_f * tokens_f, axis=-1, keepdims=True) + eps)),
        axis=0,
    )
    grad_ab = jnp.einsum("td,ct->dc", normed, dab, preferred_element_type=f32)
    ab_at, gain_at = 4 * wide, 4 * wide + 2 * heads * width
    hp_at = gain_at + DV + 2 * width
    smalls = [
        jnp.sum(dtaps, axis=1).reshape(-1),
        grad_ab.reshape(-1),
        jnp.sum(dgain, axis=0),
        grad_attn_gain_part,
        grad_mlp_gain_part,
        jnp.sum(dhp, axis=1),
    ]
    grad_normed = tie(low(grad_normed), back_up)
    payload, send, total = line_steps(grad_normed, "tp")
    came.append(next_hop(after(came[0], grad_normed), "tp", 1))
    moved = send(0, payload(0, None))
    by_seq = tree_sum(jnp.concatenate(smalls), "seq", 0)
    pair = after(payload(1, moved), by_seq, *came[1])
    came.append(next_hop(after(came[1], pair[0]), "tp", 2))
    moved = send(1, pair)
    by_all = tree_sum(by_seq[gain_at:hp_at], "tp", 0)
    moved = send(2, after(payload(2, moved), by_all, *came[2]))
    term_proj = tie(weight_grad(normed, d_all), *moved)
    grad_one = total(moved)
    block_out = assembled(block_own, came, "tp")
    grad_proj = scatter_rows(term_proj).astype(f32)
    _, norm_one_back = jax.vjp(lambda v: rms_scale(v, gain_one), mine(tokens).astype(f32))
    (grad_tokens_norm,) = norm_one_back(grad_one)
    own_grad = low(grad_middle + grad_tokens_norm)
    came = [next_hop((own_grad, own_grad), "tp", 0)]
    came.append(next_hop(came[0], "tp", 1))
    back_down = swapped(tie(grad_w_down[:, half_units:], came[0][0]), "tp", 2)
    came.append(next_hop(came[1], "tp", 2))
    grad_tokens = assembled(own_grad, came, "tp").astype(f32)

    grad_w_gate = grad_w_both[:, :units].astype(f32) + back_gate[:, :units].astype(f32)
    grad_w_up = grad_w_both[:, all_units : all_units + units].astype(f32) + back_up[:, :units].astype(f32)
    grad_w_down = grad_w_down[:, :units].astype(f32) + back_down[:, :units].astype(f32)

    rows_in = width // count
    taps_sum = by_seq[:ab_at].reshape(4, wide)
    ab_sum = lax.dynamic_slice_in_dim(
        by_seq[ab_at:gain_at].reshape(width, 2 * heads), me * rows_in, rows_in, 0
    )
    hp_sum = by_seq[hp_at:]
    own_gain = lambda at: lax.dynamic_slice_in_dim(by_all, at + me * rows_in, rows_in, 0)
    return (
        block_out,
        final_state,
        grad_tokens,
        own_gain(DV),
        grad_proj[:, :kd],
        grad_proj[:, kd : 2 * kd],
        grad_proj[:, 2 * kd : wide],
        grad_proj[:, wide:],
        ab_sum[:, :heads],
        ab_sum[:, heads:],
        taps_sum[:, :kd],
        taps_sum[:, kd : 2 * kd],
        taps_sum[:, 2 * kd :],
        hp_sum[:heads],
        hp_sum[heads:],
        by_all[:DV],
        grad_w_out.astype(f32),
        own_gain(DV + width),
        grad_w_gate,
        grad_w_up,
        grad_w_down,
    )


def solution(mesh):
    in_specs = (
        P("seq", None),
        P("seq"),
        P("seq", "tp"),
        P("seq", "tp"),
        P("seq", "tp"),
        P("seq", "tp"),
        P("seq", "tp"),
        P("seq", "tp"),
        P(None, "tp"),
        P(None, "tp"),
        P(None, "tp"),
        P("tp"),
        P("tp"),
        P(),
        P("seq", "tp"),
        P("seq"),
        P("seq", "tp"),
        P("seq", "tp"),
        P("seq", "tp"),
        P("tp", None, None),
        P(),
        P(),
        P("seq", None),
    )
    out_specs = (
        P("seq", None),
        P("tp", "seq", None),
        P("seq", None),
        P("seq"),
        P("seq", "tp"),
        P("seq", "tp"),
        P("seq", "tp"),
        P("seq", "tp"),
        P("seq", "tp"),
        P("seq", "tp"),
        P(None, "tp"),
        P(None, "tp"),
        P(None, "tp"),
        P("tp"),
        P("tp"),
        P(),
        P("seq", "tp"),
        P("seq"),
        P("seq", "tp"),
        P("seq", "tp"),
        P("seq", "tp"),
    )
    return jax.shard_map(body, mesh=mesh, in_specs=in_specs, out_specs=out_specs, check_vma=False)
```

```python
from functools import partial

import jax
import jax.numpy as jnp
from jax import lax
from jax.experimental import pallas as pl
from jax.experimental.pallas import tpu as pltpu
from jax.sharding import PartitionSpec as P

DK = 128
DV = 256
DOC_STEP = 64
BLOCK = 128
WIDE = DK + DV
eps = 1e-06
f32 = jnp.float32
bf16 = jnp.bfloat16
CLOSED = -128.0


def low(v):
    return v.astype(bf16)


def mm(a, b):
    return lax.dot_general(low(a), low(b), (((1,), (0,)), ((), ())), preferred_element_type=f32)


def mm_t(a, b):
    return lax.dot_general(low(a), low(b), (((1,), (1,)), ((), ())), preferred_element_type=f32)


def t_mm(a, b):
    return lax.dot_general(low(a), low(b), (((0,), (0,)), ((), ())), preferred_element_type=f32)


def exact_mm(a, b):
    return lax.dot_general(
        a, b, (((1,), (0,)), ((), ())), precision=lax.Precision.HIGHEST, preferred_element_type=f32
    )


def sigmoid(v):
    return 1.0 / (1.0 + jnp.exp(-v))


def square_ids():
    return (
        lax.broadcasted_iota(jnp.int32, (BLOCK, BLOCK), 0),
        lax.broadcasted_iota(jnp.int32, (BLOCK, BLOCK), 1),
    )


def softplus(v):
    return jnp.maximum(v, 0.0) + jnp.log(1.0 + jnp.exp(-jnp.abs(v)))


def decay_rows(ab, hp, keep_a, keep_b, heads):
    lane = lax.broadcasted_iota(jnp.int32, (heads, BLOCK), 1)
    opens = ((lane == 0) & (keep_a < 0.5)) | ((lane == DOC_STEP) & (keep_b < 0.5))
    moved = ab[:heads] + hp[heads:]
    log_decay = jnp.where(opens, CLOSED, -hp[:heads] * softplus(moved))
    return log_decay, sigmoid(ab[heads:]), moved, opens


def to_column(row, diag):
    return jnp.sum(jnp.where(diag, row, 0.0), axis=1, keepdims=True)


def to_row(column, diag):
    return jnp.sum(jnp.where(diag, column, 0.0), axis=0, keepdims=True)


def tap_mask(tap, keep_a, keep_b):
    row = lax.broadcasted_iota(jnp.int32, (BLOCK, DK), 0)
    inner = (row >= DOC_STEP) & (row < DOC_STEP + tap)
    return jnp.where(row < tap, keep_a, jnp.where(inner, keep_b, 1.0))


def tap_mask_back(tap, keep_b):
    row = lax.broadcasted_iota(jnp.int32, (BLOCK, DK), 0)
    return jnp.where((row >= DOC_STEP - tap) & (row < DOC_STEP), keep_b, 1.0)


def conv_total(rows_ref, taps_ref, col, masks):
    cols = slice(col, col + DK)
    total = rows_ref[8 : 8 + BLOCK, cols] * taps_ref[0:1, cols]
    for tap in range(1, 4):
        total = total + rows_ref[8 - tap : 8 - tap + BLOCK, cols] * masks[tap] * taps_ref[
            tap : tap + 1, cols
        ]
    return total


def inverse_lower(a_list, row, col):
    eye = (row == col).astype(f32)
    low_a = [low(a) for a in a_list]
    base = (row >> 3) == (col >> 3)
    x1 = [jnp.where(base, -a, 0.0) for a in a_list]
    x2 = [mm(x, x) for x in x1]
    t = [eye + x + y + mm(x, y) for x, y in zip(x1, x2)]
    x4 = [mm(x, x) for x in x2]
    t = [v + mm(v, x) for v, x in zip(t, x4)]
    for level in (3, 4, 5, 6):
        off = ((row >> (level + 1)) == (col >> (level + 1))) & ((row >> level) != (col >> level))
        part = [mm(jnp.where(off, a, 0.0), v) for a, v in zip(a_list, t)]
        t = [v - mm(v, p) for v, p in zip(t, part)]
    head = [low(v) for v in t]
    tail = [low(v - h.astype(f32)) for v, h in zip(t, head)]
    left = [eye - v - mm(a, h) - mm(a, s) for v, a, h, s in zip(t, low_a, head, tail)]
    return [v + mm(h, r) for v, h, r in zip(t, head, left)]


def load_rows(rows_ref, x_ref, halo_ref, rim_ref, first):
    rows_ref[0:8, :] = jnp.where(first, rim_ref[...], halo_ref[...])
    rows_ref[8 : 8 + BLOCK, :] = x_ref[...]


def unit(v, factor):
    scale = lax.rsqrt(jnp.sum(v * v, axis=1, keepdims=True) + eps) * factor
    return v * scale, scale


def silu(v):
    s = sigmoid(v)
    return v * s, s


def forward_kernel(
    heads,
    keep_ref,
    hp_ref,
    ab_ref,
    x_ref,
    halo_ref,
    rim_ref,
    taps_ref,
    gb_ref,
    t_ref,
    u_ref,
    w_ref,
    pre_ref,
    qf_ref,
    ob_ref,
    map_ref,
    rows_ref,
    state_ref,
):
    c = pl.program_id(0)
    hs = range(heads)
    row, col = square_ids()
    diag = row == col

    @pl.when(c == 0)
    def _():
        for h in hs:
            state_ref[h] = jnp.concatenate(
                [diag.astype(f32), jnp.zeros((DK, DV), f32)], axis=1
            )

    load_rows(rows_ref, x_ref, halo_ref, rim_ref, c == 0)
    keep_a, keep_b = keep_ref[2 * c], keep_ref[2 * c + 1]
    log_decay, beta, _, _ = decay_rows(ab_ref[...], hp_ref[...], keep_a, keep_b, heads)
    cum = exact_mm(log_decay, (row <= col).astype(f32))
    gb_ref[...] = jnp.concatenate([cum, beta], axis=0)
    masks = [None] + [tap_mask(j, keep_a, keep_b) for j in (1, 2, 3)]
    key_at, value_at = heads * DK, 2 * heads * DK

    keys = [
        unit(silu(conv_total(rows_ref, taps_ref, key_at + h * DK, masks))[0], 1.0)[0] for h in hs
    ]
    g_row = [cum[h : h + 1] for h in hs]
    g_col = [to_column(g_row[h], diag) for h in hs]
    b_col = [to_column(beta[h : h + 1], diag) for h in hs]
    decay = [jnp.exp(jnp.where(row >= col, g_col[h] - g_row[h], -1e30)) for h in hs]
    grams = [mm_t(k, k) for k in keys]
    a = [jnp.where(row > col, b_col[h] * decay[h] * grams[h], 0.0) for h in hs]
    t = [low(v) for v in inverse_lower(a, row, col)]
    values = [
        jnp.concatenate(
            [
                silu(conv_total(rows_ref, taps_ref, value_at + h * DV + s * DK, masks))[0]
                for s in range(DV // DK)
            ],
            axis=1,
        )
        for h in hs
    ]
    u = [mm(t[h], b_col[h] * values[h]) for h in hs]
    grow = [jnp.exp(g) for g in g_col]
    w = [low(mm(t[h], (b_col[h] * grow[h]) * keys[h])) for h in hs]
    queries = [
        unit(silu(conv_total(rows_ref, taps_ref, h * DK, masks))[0], DK ** (-0.5))[0] for h in hs
    ]
    scores = [low(mm_t(queries[h], keys[h]) * decay[h]) for h in hs]
    last = [cum[h : h + 1, BLOCK - 1 : BLOCK] for h in hs]
    tail = [low(jnp.exp(last[h] - g_col[h]) * keys[h]) for h in hs]
    state = [state_ref[h] for h in hs]
    low_state = [low(s) for s in state]
    fresh = [
        jnp.concatenate([jnp.zeros((BLOCK, DK), f32), u[h]], axis=1) - mm(w[h], low_state[h])
        for h in hs
    ]
    low_fresh = [low(v) for v in fresh]
    for h in hs:
        new = jnp.exp(last[h]) * state[h] + t_mm(tail[h], low_fresh[h])
        state_ref[h] = new
        map_ref[h] = low(new)
    both = [mm(grow[h] * queries[h], low_state[h]) + mm(scores[h], low_fresh[h]) for h in hs]
    for h in hs:
        t_ref[0, h] = t[h]
        u_ref[:, h * DV : (h + 1) * DV] = low(u[h])
        w_ref[:, h * DK : (h + 1) * DK] = w[h]
        pre_ref[0, h] = low_state[h]
        qf_ref[:, h * DK : (h + 1) * DK] = low(both[h][:, :DK])
        ob_ref[:, h * DV : (h + 1) * DV] = both[h][:, DK:]


def const_spec(shape):
    return pl.BlockSpec(shape, lambda c: (0,) * len(shape))


def params():
    return pltpu.CompilerParams(
        dimension_semantics=("arbitrary",), vmem_limit_bytes=56 * 1024 * 1024
    )


SMEM = pl.BlockSpec(memory_space=pltpu.SMEM)


ANY = pl.BlockSpec(memory_space=pl.ANY)


def ordered(kernel, first, extra):
    def run(*refs):
        return kernel(*refs[:first], *refs[first + extra :])

    return run


def cost(us):
    return pl.CostEstimate(
        flops=int(us * 1.0e9), bytes_accessed=int(us * 1.0e6), transcendentals=0
    )


def forward_local(keep, hp, ab, proj, rim, taps, after=()):
    heads = hp.shape[0] // 2
    length = proj.shape[0]
    blocks = length // BLOCK
    kd, vd = heads * DK, heads * DV
    width = 2 * kd + vd
    shape = jax.ShapeDtypeStruct
    return pl.pallas_call(
        ordered(partial(forward_kernel, heads), 7, len(after)),
        grid=(blocks,),
        in_specs=[
            SMEM,
            const_spec((2 * heads, BLOCK)),
            pl.BlockSpec((2 * heads, BLOCK), lambda c: (0, c)),
            pl.BlockSpec((BLOCK, width), lambda c: (c, 0)),
            pl.BlockSpec((8, width), lambda c: (jnp.maximum(c * (BLOCK // 8) - 1, 0), 0)),
            const_spec((8, width)),
            const_spec((4, width)),
        ]
        + [ANY] * len(after),
        out_specs=[
            pl.BlockSpec((2 * heads, BLOCK), lambda c: (0, c)),
            pl.BlockSpec((1, heads, BLOCK, BLOCK), lambda c: (c, 0, 0, 0)),
            pl.BlockSpec((BLOCK, vd), lambda c: (c, 0)),
            pl.BlockSpec((BLOCK, kd), lambda c: (c, 0)),
            pl.BlockSpec((1, heads, DK, WIDE), lambda c: (c, 0, 0, 0)),
            pl.BlockSpec((BLOCK, kd), lambda c: (c, 0)),
            pl.BlockSpec((BLOCK, vd), lambda c: (c, 0)),
            const_spec((heads, DK, WIDE)),
        ],
        out_shape=[
            shape((2 * heads, length), f32),
            shape((blocks, heads, BLOCK, BLOCK), bf16),
            shape((length, vd), bf16),
            shape((length, kd), bf16),
            shape((blocks, heads, DK, WIDE), bf16),
            shape((length, kd), bf16),
            shape((length, vd), f32),
            shape((heads, DK, WIDE), bf16),
        ],
        scratch_shapes=[
            pltpu.VMEM((8 + BLOCK, width), f32),
            pltpu.VMEM((heads, DK, WIDE), f32),
        ],
        compiler_params=params(),
        cost_estimate=cost(30),
        name="delta_forward",
    )(keep, hp, ab, proj, proj, rim, taps, *after)


def out_norm(ob, qf, start, gain):
    out = ob + mm(qf, start)
    inv = lax.rsqrt(jnp.mean(out * out, axis=1, keepdims=True) + eps)
    return out, inv


def gate_kernel(
    heads, place_ref, maps_ref, init_ref, ob_ref, qf_ref, gate_ref, gain_ref,
    gated_ref, start_ref, final_ref,
):
    c = pl.program_id(0)
    hs = range(heads)

    @pl.when(c == 0)
    def _():
        def step(p, states):
            return tuple(
                mm(maps_ref[p, h, :, :DK], states[h]) + maps_ref[p, h, :, DK:].astype(f32)
                for h in hs
            )

        begin = lax.fori_loop(0, place_ref[0], step, tuple(init_ref[h] for h in hs))
        for h in hs:
            start_ref[h] = begin[h]
        end = lax.fori_loop(place_ref[0], place_ref[1], step, begin)
        for h in hs:
            final_ref[h] = end[h]

    for h in hs:
        vs = slice(h * DV, (h + 1) * DV)
        out, inv = out_norm(
            ob_ref[:, vs], qf_ref[:, h * DK : (h + 1) * DK], start_ref[h], gain_ref[...]
        )
        gated_ref[:, vs] = low(out * inv * gain_ref[...] * silu(gate_ref[:, vs])[0])


def gate_forward(place, maps, init_state, ob, qf, gate_proj, gain, after=()):
    heads = init_state.shape[0]
    length, vd = ob.shape
    kd = heads * DK
    rows = 256
    shape = jax.ShapeDtypeStruct
    return pl.pallas_call(
        ordered(partial(gate_kernel, heads), 7, len(after)),
        grid=(length // rows,),
        in_specs=[
            SMEM,
            const_spec(maps.shape),
            const_spec(init_state.shape),
            pl.BlockSpec((rows, vd), lambda c: (c, 0)),
            pl.BlockSpec((rows, kd), lambda c: (c, 0)),
            pl.BlockSpec((rows, vd), lambda c: (c, gate_proj.shape[1] // vd - 1)),
            const_spec((1, DV)),
        ]
        + [ANY] * len(after),
        out_specs=[
            pl.BlockSpec((rows, vd), lambda c: (c, 0)),
            const_spec(init_state.shape),
            const_spec(init_state.shape),
        ],
        out_shape=[
            shape((length, vd), bf16),
            shape(init_state.shape, f32),
            shape(init_state.shape, f32),
        ],
        compiler_params=params(),
        cost_estimate=cost(10),
        name="gate_forward",
    )(place, maps, init_state, ob, qf, gate_proj, gain, *after)


def gate_back_kernel(
    heads, start_ref, ob_ref, qf_ref, gate_ref, gain_ref, grad_ref,
    dout_ref, dgate_ref, dgain_ref, lead_ref, total_ref,
):
    c = pl.program_id(0)

    @pl.when(c == 0)
    def _():
        dgain_ref[...] = jnp.zeros_like(dgain_ref)
        total_ref[...] = jnp.zeros_like(total_ref)

    gain = gain_ref[...]
    for h in range(heads):
        vs = slice(h * DV, (h + 1) * DV)
        qf = qf_ref[:, h * DK : (h + 1) * DK]
        out, inv = out_norm(ob_ref[:, vs], qf, start_ref[h], gain)
        gate = gate_ref[:, vs]
        act, s = silu(gate)
        grad = grad_ref[:, vs].astype(f32)
        hat = out * inv
        dn = grad * act
        dgate_ref[:, vs] = low(grad * hat * gain * (s * (1.0 + gate * (1.0 - s))))
        part = dn * hat
        rows = part.shape[0]
        dgain_ref[...] += jnp.sum(part.reshape(rows // 8, 8, DV), axis=0)
        dh = dn * gain
        dout = low(inv * (dh - hat * jnp.mean(dh * hat, axis=1, keepdims=True)))
        dout_ref[:, vs] = dout
        total_ref[h] += t_mm(qf, dout)

    @pl.when(c == pl.num_programs(0) - 1)
    def _():
        lead_ref[...] = low(total_ref[...])


def gate_backward(start, ob, qf, gate_proj, gain, grad, after=()):
    heads = start.shape[0]
    length, vd = ob.shape
    kd = heads * DK
    rows = 256
    shape = jax.ShapeDtypeStruct
    block_v = pl.BlockSpec((rows, vd), lambda c: (c, 0))
    return pl.pallas_call(
        ordered(partial(gate_back_kernel, heads), 6, len(after)),
        grid=(length // rows,),
        in_specs=[
            const_spec(start.shape),
            block_v,
            pl.BlockSpec((rows, kd), lambda c: (c, 0)),
            pl.BlockSpec((rows, vd), lambda c: (c, gate_proj.shape[1] // vd - 1)),
            const_spec((1, DV)),
            block_v,
        ]
        + [ANY] * len(after),
        out_specs=[
            block_v,
            pl.BlockSpec((rows, vd), lambda c: (c, 2 * kd // vd + 1)),
            const_spec((8, DV)),
            const_spec(start.shape),
        ],
        out_shape=[
            shape((length, vd), bf16),
            shape((length, 2 * kd + 2 * vd), bf16),
            shape((8, DV), f32),
            shape(start.shape, bf16),
        ],
        scratch_shapes=[pltpu.VMEM(start.shape, f32)],
        compiler_params=params(),
        cost_estimate=cost(11),
        name="gate_backward",
    )(start, ob, qf, gate_proj, gain, grad, *after)


def eights(v):
    return jnp.sum(v.reshape(v.shape[0] // 8, 8, v.shape[1]), axis=0)


def backward_kernel(
    heads, blocks,
    place_ref, keep_ref, hp_ref, ab_ref, x_ref, halo_ref, rim_ref, taps_ref,
    gb_ref, t_ref, u_ref, w_ref, pre_ref, dout_ref, start_ref, maps_ref, leads_ref,
    dx_ref, dlast_ref, drim_ref, dab_ref, dtaps_ref, dhp_ref,
    rows_ref, grads_ref, dstate_ref,
):
    step = pl.program_id(0)
    c = blocks - 1 - step
    hs = range(heads)
    row, col = square_ids()
    diag = row == col
    key_at, value_at = heads * DK, 2 * heads * DK

    @pl.when(step == 0)
    def _():
        me, count = place_ref[0], place_ref[1]

        def relay(i, grads):
            p = count - 1 - i
            return tuple(
                t_mm(maps_ref[p, h, :, :DK], grads[h]) + leads_ref[p - me - 1, h].astype(f32) for h in hs
            )

        end = lax.fori_loop(
            0, count - 1 - me, relay, tuple(jnp.zeros((DK, DV), f32) for h in hs)
        )
        for h in hs:
            dstate_ref[h] = end[h]
        grads_ref[BLOCK:, :] = jnp.zeros_like(grads_ref[BLOCK:, :])
        dtaps_ref[...] = jnp.zeros_like(dtaps_ref)
        dhp_ref[...] = jnp.zeros_like(dhp_ref)

    load_rows(rows_ref, x_ref, halo_ref, rim_ref, c == 0)
    keep_a, keep_b = keep_ref[2 * c], keep_ref[2 * c + 1]
    log_decay, beta, moved, opens = decay_rows(ab_ref[...], hp_ref[...], keep_a, keep_b, heads)
    cum = gb_ref[:heads]
    masks = [None] + [tap_mask(j, keep_a, keep_b) for j in (1, 2, 3)]
    masks_back = [None] + [tap_mask_back(j, keep_b) for j in (1, 2, 3)]

    q_sum = [conv_total(rows_ref, taps_ref, h * DK, masks) for h in hs]
    k_sum = [conv_total(rows_ref, taps_ref, key_at + h * DK, masks) for h in hs]
    q_act = [silu(v) for v in q_sum]
    k_act = [silu(v) for v in k_sum]
    q_unit = [unit(v[0], DK ** (-0.5)) for v in q_act]
    k_unit = [unit(v[0], 1.0) for v in k_act]
    queries = [v[0] for v in q_unit]
    keys = [v[0] for v in k_unit]
    low_q = [low(v) for v in queries]
    low_k = [low(v) for v in keys]
    g_row = [cum[h : h + 1] for h in hs]
    g_col = [to_column(g_row[h], diag) for h in hs]
    b_col = [to_column(beta[h : h + 1], diag) for h in hs]
    grow = [jnp.exp(v) for v in g_col]
    last = [cum[h : h + 1, BLOCK - 1 : BLOCK] for h in hs]
    tail = [jnp.exp(last[h] - g_col[h]) for h in hs]
    decay = [jnp.exp(jnp.where(row >= col, g_col[h] - g_row[h], -1e30)) for h in hs]
    grams = [mm_t(k, k) for k in low_k]
    raw = [mm_t(low_q[h], low_k[h]) for h in hs]
    scores = [low(raw[h] * decay[h]) for h in hs]
    begin = [low(start_ref[h]) for h in hs]
    state = [
        mm(pre_ref[0, h, :, :DK], begin[h]) + pre_ref[0, h, :, DK:].astype(f32) for h in hs
    ]
    low_state = [low(v) for v in state]
    u = [u_ref[:, h * DV : (h + 1) * DV] for h in hs]
    w = [w_ref[:, h * DK : (h + 1) * DK] for h in hs]
    t = [t_ref[0, h] for h in hs]
    fresh = [low(u[h].astype(f32) - mm(w[h], low_state[h])) for h in hs]
    dout = [dout_ref[:, h * DV : (h + 1) * DV] for h in hs]
    dstate = [dstate_ref[h] for h in hs]
    low_dstate = [low(v) for v in dstate]
    key_tail = [tail[h] * keys[h] for h in hs]
    dfresh = [t_mm(scores[h], dout[h]) + mm(key_tail[h], low_dstate[h]) for h in hs]
    low_df = [low(v) for v in dfresh]
    q_grow = [grow[h] * queries[h] for h in hs]
    for h in hs:
        dstate_ref[h] = (
            jnp.exp(last[h]) * dstate[h] + t_mm(q_grow[h], dout[h]) - t_mm(w[h], low_df[h])
        )
    dscores = [mm_t(dout[h], fresh[h]) for h in hs]
    dq_grow = [mm_t(dout[h], low_state[h]) for h in hs]
    dk_tail = [mm_t(fresh[h], low_dstate[h]) for h in hs]
    dw = [-mm_t(low_df[h], low_state[h]) for h in hs]
    r_value = [t_mm(t[h], low_df[h]) for h in hs]
    r_key = [t_mm(t[h], dw[h]) for h in hs]
    da = [
        jnp.where(row > col, -(mm_t(r_value[h], u[h]) + mm_t(r_key[h], w[h])), 0.0) for h in hs
    ]
    dsd = [dscores[h] * decay[h] for h in hs]
    dad = [da[h] * decay[h] for h in hs]
    mixed = [dad[h] * grams[h] for h in hs]
    both = [b_col[h] * mixed[h] + dsd[h] * raw[h] for h in hs]
    lift = [b_col[h] * grow[h] for h in hs]
    low_dsd = [low(v) for v in dsd]
    hmat = [b_col[h] * dad[h] for h in hs]
    dq = [grow[h] * dq_grow[h] + mm(low_dsd[h], low_k[h]) for h in hs]
    dk = [
        t_mm(low_dsd[h], low_q[h])
        + tail[h] * dk_tail[h]
        + lift[h] * r_key[h]
        + mm(hmat[h], low_k[h])
        + t_mm(hmat[h], low_k[h])
        for h in hs
    ]

    cum_parts, beta_parts = [], []
    for h in hs:
        rk = jnp.sum(r_key[h] * keys[h], axis=1, keepdims=True)
        tails = jnp.sum(dk_tail[h] * key_tail[h], axis=1, keepdims=True)
        part = (
            jnp.sum(both[h], axis=1, keepdims=True)
            + jnp.sum(dq_grow[h] * q_grow[h], axis=1, keepdims=True)
            + lift[h] * rk
            - tails
        )
        end_part = jnp.sum(tails, axis=0, keepdims=True) + jnp.exp(last[h]) * jnp.sum(
            jnp.sum(dstate[h] * state[h], axis=1, keepdims=True), axis=0, keepdims=True
        )
        dcum = to_row(part, diag) - jnp.sum(both[h], axis=0, keepdims=True)
        lane = lax.broadcasted_iota(jnp.int32, (1, BLOCK), 1)
        cum_parts.append(dcum + jnp.where(lane == BLOCK - 1, end_part, 0.0))
        beta_parts.append(
            jnp.sum(mixed[h], axis=1, keepdims=True) + grow[h] * rk
        )

    def conv_back(dact, total, s, at):
        dtot = dact * (s * (1.0 + total * (1.0 - s)))
        cols = slice(at, at + DK)
        grads_ref[0:BLOCK, cols] = dtot
        dtaps_ref[0, :, cols] += eights(dtot * rows_ref[8 : 8 + BLOCK, cols])
        dx = dtot * taps_ref[0:1, cols]
        for j in (1, 2, 3):
            dtaps_ref[j, :, cols] += eights(
                dtot * masks[j] * rows_ref[8 - j : 8 - j + BLOCK, cols]
            )
            dx = dx + grads_ref[j : j + BLOCK, cols] * masks_back[j] * taps_ref[j : j + 1, cols]
        dx_ref[:, cols] = low(dx)

        @pl.when(step == 0)
        def _():
            dlast_ref[:, cols] = dx[BLOCK - 8 :]

        grads_ref[BLOCK : BLOCK + 8, cols] = dtot[0:8] * keep_a

    def unit_back(grad, normal, scale, factor):
        inner = jnp.sum(grad * normal, axis=1, keepdims=True) * (1.0 / (factor * factor))
        return scale * (grad - normal * inner)

    for h in hs:
        conv_back(
            unit_back(dq[h], queries[h], q_unit[h][1], DK ** (-0.5)),
            q_sum[h], q_act[h][1], h * DK,
        )
        conv_back(
            unit_back(dk[h], keys[h], k_unit[h][1], 1.0), k_sum[h], k_act[h][1], key_at + h * DK
        )
        dot_v = 0.0
        for s in range(DV // DK):
            at = value_at + h * DV + s * DK
            total = conv_total(rows_ref, taps_ref, at, masks)
            act, sig = silu(total)
            rv = r_value[h][:, s * DK : (s + 1) * DK]
            dot_v = dot_v + jnp.sum(rv * act, axis=1, keepdims=True)
            conv_back(b_col[h] * rv, total, sig, at)
        beta_parts[h] = to_row(beta_parts[h] + dot_v, diag)

    dcum = jnp.concatenate(cum_parts, axis=0)
    dlog = jnp.where(opens, 0.0, exact_mm(dcum, (row >= col).astype(f32)))
    dbeta = jnp.concatenate(beta_parts, axis=0)
    dalpha = -dlog * hp_ref[:heads] * sigmoid(moved)
    dab_ref[...] = jnp.concatenate([dalpha, dbeta * beta * (1.0 - beta)], axis=0)
    dhp_ref[...] += jnp.concatenate([-dlog * softplus(moved), dalpha], axis=0)

    @pl.when(step == blocks - 1)
    def _():
        grads_ref[BLOCK - 8 : BLOCK, :] = jnp.zeros((8, grads_ref.shape[1]), f32)
        total = jnp.zeros((8, grads_ref.shape[1]), f32)
        for j in (1, 2, 3):
            total = total + grads_ref[BLOCK - 8 + j : BLOCK + j, :] * taps_ref[j : j + 1, :]
        drim_ref[...] = total


def backward_local(
    place, keep, hp, ab, proj, rim, taps, gb, t, u, w, pre, dout, start, maps, leads, grads,
    after=(),
):
    heads = hp.shape[0] // 2
    length = proj.shape[0]
    blocks = length // BLOCK
    kd, vd = heads * DK, heads * DV
    width = 2 * kd + vd
    shape = jax.ShapeDtypeStruct
    back = blocks - 1
    eighth = BLOCK // 8
    return pl.pallas_call(
        ordered(partial(backward_kernel, heads, blocks), 17, 1 + len(after)),
        grid=(blocks,),
        in_specs=[
            SMEM,
            SMEM,
            const_spec((2 * heads, BLOCK)),
            pl.BlockSpec((2 * heads, BLOCK), lambda c: (0, back - c)),
            pl.BlockSpec((BLOCK, width), lambda c: (back - c, 0)),
            pl.BlockSpec((8, width), lambda c: (jnp.maximum((back - c) * eighth - 1, 0), 0)),
            const_spec((8, width)),
            const_spec((4, width)),
            pl.BlockSpec((2 * heads, BLOCK), lambda c: (0, back - c)),
            pl.BlockSpec((1, heads, BLOCK, BLOCK), lambda c: (back - c, 0, 0, 0)),
            pl.BlockSpec((BLOCK, vd), lambda c: (back - c, 0)),
            pl.BlockSpec((BLOCK, kd), lambda c: (back - c, 0)),
            pl.BlockSpec((1, heads, DK, WIDE), lambda c: (back - c, 0, 0, 0)),
            pl.BlockSpec((BLOCK, vd), lambda c: (back - c, 0)),
            const_spec(start.shape),
            const_spec(maps.shape),
            const_spec(leads.shape),
        ]
        + [ANY] * (1 + len(after)),
        out_specs=[
            pl.BlockSpec((BLOCK, width), lambda c: (back - c, 0)),
            const_spec((8, width)),
            const_spec((8, width)),
            pl.BlockSpec((2 * heads, BLOCK), lambda c: (0, back - c)),
            const_spec((4, 8, width)),
            const_spec((2 * heads, BLOCK)),
        ],
        out_shape=[
            shape(grads.shape, bf16),
            shape((8, width), f32),
            shape((8, width), f32),
            shape((2 * heads, length), f32),
            shape((4, 8, width), f32),
            shape((2 * heads, BLOCK), f32),
        ],
        scratch_shapes=[
            pltpu.VMEM((8 + BLOCK, width), f32),
            pltpu.VMEM((8 + BLOCK, width), f32),
            pltpu.VMEM(start.shape, f32),
        ],
        compiler_params=params(),
        input_output_aliases={17: 0},
        cost_estimate=cost(50),
        name="delta_backward",
    )(
        place, keep, hp, ab, proj, proj, rim, taps, gb, t, u, w, pre, dout, start, maps, leads,
        grads, *after,
    )


def tie(block, *after):
    return pl.pallas_call(
        lambda *refs: None,
        in_specs=[ANY] * (1 + len(after)),
        out_specs=ANY,
        out_shape=jax.ShapeDtypeStruct(block.shape, block.dtype),
        input_output_aliases={0: 0},
        cost_estimate=cost(1),
        name="tie",
    )(block, *after)


def swiglu_kernel(units, gate_ref, up_ref, grad_ref, hidden_ref, grads_ref):
    gate, up = gate_ref[...].astype(f32), up_ref[...].astype(f32)
    act, s = silu(gate)
    hidden_ref[...] = low(act * up)
    grad = grad_ref[...].astype(f32)
    grads_ref[:, :units] = low(grad * up * (s * (1.0 + gate * (1.0 - s))))
    grads_ref[:, units:] = low(grad * act)


def swiglu_both(gate, up, grad):
    rows, units = grad.shape
    step = 64
    spec = lambda columns: pl.BlockSpec((step, columns), lambda c: (c, 0))
    shape = jax.ShapeDtypeStruct
    return pl.pallas_call(
        partial(swiglu_kernel, units),
        grid=(rows // step,),
        in_specs=[spec(units)] * 3,
        out_specs=[spec(units), spec(2 * units)],
        out_shape=[shape((rows, units), bf16), shape((rows, 2 * units), bf16)],
        compiler_params=params(),
        cost_estimate=cost(8),
        name="swiglu_both",
    )(gate, up, grad)


def rms_scale(values, scales):
    return (
        values * lax.rsqrt(jnp.mean(values * values, axis=-1, keepdims=True) + eps) * scales
    )


def doc_numbers(positions, seg_starts, continues):
    opens = 1 - continues
    passed = (positions[:, None] >= seg_starts[None, 1:]).astype(jnp.int32)
    return jnp.sum(passed * opens[None, :], axis=1)


def passed_along(block, axis, distance):
    devices = range(lax.axis_size(axis))
    route = [(i - distance, i) for i in devices if i - distance in devices]
    return lax.ppermute(block, axis, route)


def rows_times(left, right):
    return jnp.dot(left, right, preferred_element_type=f32)


def times_back(left, right):
    return jnp.einsum("tc,dc->td", left, right, preferred_element_type=f32)


def weight_grad(left, right):
    return low(jnp.einsum("td,tc->dc", left, right, preferred_element_type=f32))


def gather_rows(block, axis="seq"):
    return lax.all_gather(block, axis, axis=0, tiled=True)


def scatter_rows(block, axis="seq"):
    return lax.psum_scatter(low(block), axis, scatter_dimension=0, tiled=True)


def next_hop(pair, axis, step):
    n = lax.axis_size(axis)
    return (
        lax.ppermute(pair[0], axis, [(i, i + 1) for i in range(step, n - 1)]),
        lax.ppermute(pair[1], axis, [(n - 1 - i, n - 2 - i) for i in range(step, n - 1)]),
    )


def line_steps(rows, axis):
    n = lax.axis_size(axis)
    me = lax.axis_index(axis)
    own = rows.shape[0] // n
    chunk = lambda at: lax.dynamic_slice_in_dim(rows, jnp.clip(at, 0, n - 1) * own, own, 0)

    def payload(step, came):
        up, down = chunk(n - 1 + me - step), chunk(me - (n - 1) + step)
        if came is None:
            return up, down
        return low(up.astype(f32) + came[0].astype(f32)), low(
            down.astype(f32) + came[1].astype(f32)
        )

    def send(step, pair):
        return (
            lax.ppermute(pair[0], axis, [(i, i + 1) for i in range(step + 1)]),
            lax.ppermute(pair[1], axis, [(n - 1 - i, n - 2 - i) for i in range(step + 1)]),
        )

    return payload, send, lambda came: (
        chunk(me).astype(f32) + came[0].astype(f32) + came[1].astype(f32)
    )


def line_scatter(rows, axis):
    payload, send, total = line_steps(rows, axis)
    came = None
    for step in range(lax.axis_size(axis) - 1):
        came = send(step, payload(step, came))
    return total(came)


def assembled(block, came, axis):
    n = lax.axis_size(axis)
    me = lax.axis_index(axis)
    own = block.shape[0]
    out = jnp.zeros((n * own,) + block.shape[1:], block.dtype)
    put = lambda out, part, at: lax.dynamic_update_slice_in_dim(
        out, part, jnp.clip(at, 0, n - 1) * own, 0
    )
    for step in range(n - 2, -1, -1):
        right, left = came[step]
        out = put(put(out, right, me - 1 - step), left, me + 1 + step)
    return put(out, block, me)


def line_gather(block, axis):
    came = [(block, block)]
    for step in range(lax.axis_size(axis) - 1):
        came.append(next_hop(came[-1], axis, step))
    return assembled(block, came[1:], axis)


def swapped(block, axis, bit):
    return lax.ppermute(block, axis, [(i, i ^ bit) for i in range(lax.axis_size(axis))])


def exchange_step(values, axis, step):
    return values + swapped(values, axis, 1 << step)


def tree_sum(values, axis, first):
    for step in range(first, lax.axis_size(axis).bit_length() - 1):
        values = exchange_step(values, axis, step)
    return values


def body(
    tokens, attn_gain, w_query, w_key, w_value, w_gate_out, w_alpha, w_beta,
    conv_query, conv_key, conv_value, decay_scale, dt_bias, out_gain, w_out, mlp_gain,
    w_mlp_gate, w_mlp_up, w_mlp_down, init_state, seg_starts, continues, cotangent,
):
    count = lax.axis_size("seq")
    me = lax.axis_index("seq")
    lane = lax.axis_index("tp")
    length, width = tokens.shape
    heads = decay_scale.shape[0]
    kd, vd = heads * DK, heads * DV
    own = length // lax.axis_size("tp")
    rows_of = lambda rows, at: lax.dynamic_slice_in_dim(rows, at * own, own, 0)
    mine = lambda rows: rows_of(rows, lane)
    pair = lambda rows: jnp.concatenate([rows_of(rows, lane), rows_of(rows, lane ^ 1)], axis=0)

    after = lambda pair, *awaited: [tie(v, *awaited) for v in pair]

    units = w_mlp_gate.shape[1]
    fill = jnp.zeros((w_mlp_gate.shape[0], -units % 128), bf16)
    half_units = units + fill.shape[1]
    all_units = 2 * half_units
    other_down = swapped(w_mlp_down, "tp", 2)
    other_gate = swapped(w_mlp_gate, "tp", 2)
    first_part = units * 2 // 7 // 128 * 128
    other_up = [
        swapped(w_mlp_up[:, :first_part], "tp", 2),
        swapped(w_mlp_up[:, first_part:], "tp", 2),
    ]
    small = gather_rows(
        jnp.concatenate(
            [w_alpha, w_beta, attn_gain[:, None], mlp_gain[:, None]]
            + [jnp.zeros((w_alpha.shape[0], 6), bf16)],
            axis=1,
        )
    )
    full_ab = small[:, : 2 * heads]
    gain_one = small[:, 2 * heads].astype(f32)
    gain_two = small[:, 2 * heads + 1].astype(f32)
    full_qkv = gather_rows(jnp.concatenate([w_query, w_key, w_value], axis=1))
    full_go = gather_rows(jnp.concatenate([w_gate_out, w_out], axis=1))
    full_gate, full_out = full_go[:, :vd], full_go[:, vd:]
    full_dg = gather_rows(
        jnp.concatenate(
            [w_mlp_down, fill, other_down, fill, w_mlp_gate, fill, other_gate, fill], axis=1
        )
    )
    full_down, full_mlp_gate = full_dg[:, :all_units], full_dg[:, all_units:]

    firsts = me * length + DOC_STEP * jnp.arange(length // DOC_STEP, dtype=jnp.int32)
    keep = (
        doc_numbers(firsts, seg_starts, continues)
        == doc_numbers(firsts - 1, seg_starts, continues)
    ).astype(f32)
    place = jnp.stack([me, jnp.int32(count)]).astype(jnp.int32)
    hp = jnp.broadcast_to(jnp.concatenate([decay_scale, dt_bias])[:, None], (2 * heads, BLOCK))
    taps = jnp.concatenate([conv_query, conv_key, conv_value], axis=1)
    gain_row = out_gain[None, :]

    normed = low(rms_scale(tokens.astype(f32), gain_one))
    proj = rows_times(normed, full_qkv)
    ab = jnp.einsum("dc,td->ct", full_ab, normed, preferred_element_type=f32)
    gate_proj = rows_times(normed, full_gate)
    rim = passed_along(proj[-8:], "seq", 1)
    gb, t_inv, u, w, pre, qf, ob, own_map = forward_local(
        keep, hp, ab, proj, rim, taps, (other_down, other_gate, other_up[0])
    )
    maps = lax.all_gather(own_map, "seq", axis=0)
    gated, start, final = gate_forward(
        place, maps, init_state, ob, qf, gate_proj, gain_row
    )
    full_mlp_up = gather_rows(jnp.concatenate([w_mlp_up, fill, *other_up, fill], axis=1))
    piece = final.shape[1] // count
    final_state = lax.dynamic_slice_in_dim(final, me * piece, piece, 1)

    middle = mine(tokens).astype(f32) + line_scatter(low(times_back(gated, full_out)), "tp")
    normed_two_f, norm_two_back = jax.vjp(rms_scale, middle, gain_two)
    own_two = low(normed_two_f)
    normed_two = jnp.concatenate([own_two, swapped(own_two, "tp", 1)], axis=0)
    cot_pair = pair(cotangent)
    grad_hidden = low(rows_times(cot_pair, full_down))
    gate_mlp = low(rows_times(normed_two, full_mlp_gate))
    up_mlp = low(rows_times(tie(normed_two, gate_mlp, grad_hidden), full_mlp_up))
    hidden, grad_both = swiglu_both(gate_mlp, up_mlp, grad_hidden)
    grad_two_part = times_back(grad_both[:, :all_units], full_mlp_gate) + times_back(
        grad_both[:, all_units:], full_mlp_up
    )
    part_two = low(grad_two_part[own:])
    part_two = swapped(part_two, "tp", 1)
    grad_two = grad_two_part[:own] + part_two.astype(f32)
    term_both = tie(weight_grad(normed_two, grad_both), part_two)
    grad_middle_norm, grad_mlp_gain_part = norm_two_back(grad_two)
    grad_middle = mine(cotangent).astype(f32) + grad_middle_norm
    own_attn = tie(low(grad_middle), term_both)
    grad_w_both = scatter_rows(term_both)
    mlp_part = times_back(hidden, full_down)
    part_back = low(mlp_part[own:])
    term_down = weight_grad(cot_pair, hidden)
    came = [next_hop((own_attn, own_attn), "tp", 0)]
    came.append(next_hop(after(came[0], part_back), "tp", 1))
    came.append(next_hop(after(came[1], term_down), "tp", 2))
    grad_attn = assembled(own_attn, came, "tp")

    grad_gated = rows_times(grad_attn, full_out)
    dout, d_all, dgain, lead = gate_backward(
        start, ob, qf, gate_proj, gain_row, grad_gated, (part_back, term_down)
    )
    leads = [passed_along(lead, "seq", -d) for d in range(1, count)]
    grad_w_down = scatter_rows(term_down)
    term_out = weight_grad(tie(grad_attn, leads[0]), gated)
    grad_w_out = scatter_rows(term_out)
    part_back = swapped(tie(part_back, grad_attn), "tp", 1)
    block_own = low(middle + mlp_part[:own] + part_back.astype(f32))
    d_all, dlast, drim, dab, dtaps, dhp = backward_local(
        place, keep, hp, ab, proj, rim, taps, gb, t_inv, u, w, pre, dout, start, maps,
        jnp.stack(leads),
        d_all, (term_out, block_own),
    )
    came = [next_hop((block_own, block_own), "tp", 0)]
    back_gate = swapped(grad_w_both[:, half_units:all_units], "tp", 2)
    d_all = tie(d_all, *came[0], back_gate)
    back_up = swapped(tie(grad_w_both[:, all_units + half_units :], d_all), "tp", 2)

    fixed = low(dlast + passed_along(drim, "seq", -1))
    d_all = lax.dynamic_update_slice(d_all, fixed, (length - 8, 0))
    dab = low(dab)
    wide = taps.shape[1]
    grad_normed = (
        times_back(d_all[:, :wide], full_qkv)
        + times_back(d_all[:, wide:], full_gate)
        + jnp.einsum("ct,dc->td", dab, full_ab, preferred_element_type=f32)
    )
    tokens_f = tokens.astype(f32)
    grad_attn_gain_part = jnp.sum(
        grad_normed
        * (tokens_f * lax.rsqrt(jnp.mean(tokens_f * tokens_f, axis=-1, keepdims=True) + eps)),
        axis=0,
    )
    grad_normed = tie(low(grad_normed), back_up)
    grad_ab = jnp.einsum(
        "td,ct->dc", normed, tie(dab, grad_normed), preferred_element_type=f32
    )
    ab_at, gain_at = 4 * wide, 4 * wide + 2 * heads * width
    hp_at = gain_at + DV + 2 * width
    smalls = [
        jnp.sum(dtaps, axis=1).reshape(-1),
        grad_ab.reshape(-1),
        jnp.sum(dgain, axis=0),
        grad_attn_gain_part,
        grad_mlp_gain_part,
        jnp.sum(dhp, axis=1),
    ]
    payload, send, total = line_steps(grad_normed, "tp")
    came.append(next_hop(after(came[0], grad_normed), "tp", 1))
    moved = send(0, payload(0, None))
    by_seq = exchange_step(exchange_step(jnp.concatenate(smalls), "seq", 0), "seq", 1)
    pair = after(payload(1, moved), by_seq, *came[1])
    came.append(next_hop(after(came[1], pair[0]), "tp", 2))
    moved = send(1, pair)
    by_seq = tree_sum(tie(by_seq, pair[0]), "seq", 2)
    moved = send(2, after(payload(2, moved), by_seq, *came[2]))
    term_proj = tie(weight_grad(normed, d_all), *moved)
    grad_one = total(moved)
    block_out = assembled(block_own, came, "tp")
    grad_proj = scatter_rows(term_proj).astype(f32)
    _, norm_one_back = jax.vjp(lambda v: rms_scale(v, gain_one), mine(tokens).astype(f32))
    (grad_tokens_norm,) = norm_one_back(grad_one)
    own_grad = low(grad_middle + grad_tokens_norm)
    came = [next_hop((own_grad, own_grad), "tp", 0)]
    came.append(next_hop(came[0], "tp", 1))
    came.append(next_hop(came[1], "tp", 2))
    back_down = swapped(tie(grad_w_down[:, half_units:], came[2][0]), "tp", 2)
    by_seq, back_gate, back_up, grad_w_out = (
        tie(v, came[0][0]) for v in (by_seq, back_gate, back_up, grad_w_out)
    )
    by_all = tree_sum(tie(by_seq[gain_at:hp_at], came[1][0]), "tp", 0)
    grad_tokens = assembled(own_grad, came, "tp").astype(f32)

    grad_w_gate = grad_w_both[:, :units].astype(f32) + back_gate[:, :units].astype(f32)
    grad_w_up = grad_w_both[:, all_units : all_units + units].astype(f32) + back_up[:, :units].astype(f32)
    grad_w_down = grad_w_down[:, :units].astype(f32) + back_down[:, :units].astype(f32)

    rows_in = width // count
    taps_sum = by_seq[:ab_at].reshape(4, wide)
    ab_sum = lax.dynamic_slice_in_dim(
        by_seq[ab_at:gain_at].reshape(width, 2 * heads), me * rows_in, rows_in, 0
    )
    hp_sum = by_seq[hp_at:]
    own_gain = lambda at: lax.dynamic_slice_in_dim(by_all, at + me * rows_in, rows_in, 0)
    return (
        block_out,
        final_state,
        grad_tokens,
        own_gain(DV),
        grad_proj[:, :kd],
        grad_proj[:, kd : 2 * kd],
        grad_proj[:, 2 * kd : wide],
        grad_proj[:, wide:],
        ab_sum[:, :heads],
        ab_sum[:, heads:],
        taps_sum[:, :kd],
        taps_sum[:, kd : 2 * kd],
        taps_sum[:, 2 * kd :],
        hp_sum[:heads],
        hp_sum[heads:],
        by_all[:DV],
        grad_w_out.astype(f32),
        own_gain(DV + width),
        grad_w_gate,
        grad_w_up,
        grad_w_down,
    )


def solution(mesh):
    in_specs = (
        P("seq", None),
        P("seq"),
        P("seq", "tp"),
        P("seq", "tp"),
        P("seq", "tp"),
        P("seq", "tp"),
        P("seq", "tp"),
        P("seq", "tp"),
        P(None, "tp"),
        P(None, "tp"),
        P(None, "tp"),
        P("tp"),
        P("tp"),
        P(),
        P("seq", "tp"),
        P("seq"),
        P("seq", "tp"),
        P("seq", "tp"),
        P("seq", "tp"),
        P("tp", None, None),
        P(),
        P(),
        P("seq", None),
    )
    out_specs = (
        P("seq", None),
        P("tp", "seq", None),
        P("seq", None),
        P("seq"),
        P("seq", "tp"),
        P("seq", "tp"),
        P("seq", "tp"),
        P("seq", "tp"),
        P("seq", "tp"),
        P("seq", "tp"),
        P(None, "tp"),
        P(None, "tp"),
        P(None, "tp"),
        P("tp"),
        P("tp"),
        P(),
        P("seq", "tp"),
        P("seq"),
        P("seq", "tp"),
        P("seq", "tp"),
        P("seq", "tp"),
    )
    return jax.shard_map(body, mesh=mesh, in_specs=in_specs, out_specs=out_specs, check_vma=False)
```
